128 devices in a mesh: dp: 8 (over y, x_lo), tensor: 16 (over z, x_hi, core).
Axes of the slice: x: 4 (x_hi: 2, x_lo: 2; x = x_hi * 2 + x_lo), y: 4, z: 4, core: 2. Of those that a mesh axis runs over, the one named last changes fastest.
Arguments:
- context: bfloat16 [4096, 8192], P('dp', 'tensor'), may hold values from -6 to 6
- residual: bfloat16 [4096, 5120], P(('dp', 'tensor')), may hold values from -6 to 6
- out_proj: bfloat16 [8192, 5120], P('tensor'), may hold values from -0.0625 to 0.0625
- final_gain: bfloat16 [5120], replicated, may hold values from 0.099609375 to 1.8984375
- next_ids: int32 [2, 4096], P(None, ('dp', 'tensor')), may hold values from 0 to 76031, as said below
- embed_table: bfloat16 [76032, 5120], P('tensor', 'dp'), may hold values from -6 to 6
- head_weight: bfloat16 [2, 5120, 5120], P(None, None, 'tensor'), may hold values from -0.078125 to 0.078125
- state_grad: float32 [2, 4096, 5120], P(None, ('dp', 'tensor')), may hold values from -0.25 to 0.25
Outputs:
- states: bfloat16 [2, 4096, 5120], P(None, ('dp', 'tensor'))
- head_grad: float32 [2, 5120, 5120], P(None, 'dp', 'tensor')
The draws below stay inside these ranges and needn't reach their ends.
Inputs may be any that keep to these rules, and one draw needn't show every extreme that they name: `next_ids`: among the ids held by all devices that share one index of tensor, each block of 4752 consecutive ids is named at most 64 times, and one such block exactly 64 times.
All inputs are finite; a program needn't handle non-finite values.
Results may differ from the reference program's by a relative error of at most 0.025.
Values may be sent and summed in bfloat16 or wider, within the bound.
No kernel may reach another device: no remote copies, remote signals or barrier semaphores. Data moves between devices by JAX's collectives and lax.ppermute only.
A program may use at most 128 MiB of HBM per device.

```python
import jax
import jax.numpy as jnp
from jax import lax

D = 5120
QDIM = 8192
HEADS = 2
TOK_DEV = 32
VOCAB_SH = 4752
TOKENS = 4096
VOCAB = 76032
BLOCK_IDS = 512
CAP = 64
N_DP = 8
N_TENSOR = 16


def draw_next_ids(key, part):
    key = jax.random.fold_in(key, 11)
    key_plant, key_pool, key_place, key_rows = jax.random.split(key, 4)
    blocks = N_TENSOR
    per_block = BLOCK_IDS
    capacity = CAP
    planted = jax.random.randint(key_plant, (blocks,), 0, blocks)
    owner_pool = jnp.arange(capacity * (blocks - 1), dtype=jnp.int32) % (blocks - 1)
    pool_keys = jax.random.split(key_pool, blocks)
    shuffled = jax.vmap(jax.random.permutation, in_axes=(0, None))(pool_keys, owner_pool)
    shuffled = shuffled[:, :per_block - capacity]
    others = (planted[:, None] + 1 + shuffled) % blocks
    owners = jnp.concatenate([jnp.broadcast_to(planted[:, None], (blocks, capacity)), others], axis=1)
    place_keys = jax.random.split(key_place, blocks)
    owners = jax.vmap(jax.random.permutation)(place_keys, owners)
    vocab_rows = jax.random.randint(key_rows, (blocks, per_block), 0, VOCAB_SH)
    tok_ids = owners * VOCAB_SH + vocab_rows
    tok_ids = tok_ids.reshape(blocks, HEADS, N_DP, TOK_DEV).transpose(1, 2, 0, 3).reshape(HEADS, TOKENS)
    return tok_ids.astype(jnp.int32)


def shard_levels(key, extent, cuts, low, high):
    def one(axis_at, parts):
        draws = jax.random.uniform(jax.random.fold_in(jax.random.fold_in(key, 6), axis_at), (parts,), jnp.float32, low / len(cuts), high / len(cuts))
        return jnp.repeat(jnp.exp(draws), extent[axis_at] // parts).reshape((-1,) + (1,) * (len(extent) - axis_at - 1))

    level = one(*cuts[0])
    for cut in cuts[1:]:
        level = level * one(*cut)
    return level


def normal_values(own_key, extent, deviation, bound, cuts=(), kind=jnp.bfloat16):
    values = deviation * jax.random.normal(own_key, extent, jnp.float32)
    if cuts:
        values = values * shard_levels(own_key, extent, cuts, -0.22, 0.18)
    return jnp.clip(values, -bound, bound).astype(kind)


def setup_inputs(seed: int = 0) -> dict:
    key_of = jax.random.split(jax.random.key(seed), 9)
    return {
        "context": normal_values(key_of[0], (TOKENS, QDIM), 1.0, 6.0, ((0, 8), (1, 16))),
        "residual": normal_values(key_of[1], (TOKENS, D), 1.0, 6.0, ((0, 128),)),
        "out_proj": normal_values(key_of[2], (QDIM, D), QDIM ** -0.5, 0.0625, ((0, 16),)),
        "final_gain": jnp.clip(1.0 + 0.18 * jax.random.normal(key_of[3], (D,), jnp.float32), 0.099609375, 1.8984375).astype(jnp.bfloat16),
        "next_ids": draw_next_ids(jax.random.fold_in(key_of[8], 71), 0),
        "embed_table": normal_values(key_of[5], (VOCAB, D), 1.0, 6.0, ((0, 16), (1, 8))),
        "head_weight": normal_values(key_of[6], (HEADS, D, D), D ** -0.5, 0.078125, ((2, 16),)),
        "state_grad": normal_values(key_of[7], (HEADS, TOKENS, D), (TOKENS ** -0.5), 0.25, ((1, 128),), jnp.float32),
    }


norm_eps = 1e-06

def rms_scale(values):
    return lax.rsqrt(lax.optimization_barrier(jnp.mean(values * values, axis=-1, keepdims=True)) + norm_eps)

def silu_slope(pre_act):
    sigmoid = jax.nn.sigmoid(pre_act)
    return sigmoid * (1.0 + pre_act * (1.0 - sigmoid))

def round_trip(values):
    return lax.optimization_barrier(values.astype(jnp.bfloat16)).astype(jnp.float32)

def reference(context, residual, out_proj, final_gain, next_ids, embed_table, head_weight, state_grad):
    q_block = QDIM // N_TENSOR
    c_block = D // N_TENSOR
    group_rows = TOKENS // N_DP

    def add_target(block_index, running):
        ctx_part = lax.dynamic_slice_in_dim(context, block_index * q_block, q_block, 1)
        w_part = lax.dynamic_slice_in_dim(out_proj, block_index * q_block, q_block, 0)
        return running + round_trip(jnp.dot(ctx_part, w_part, preferred_element_type=jnp.float32))
    projected = lax.fori_loop(0, N_TENSOR, add_target, jnp.zeros((TOKENS, D), jnp.float32))
    hidden = residual.astype(jnp.float32) + projected
    current = hidden * rms_scale(hidden) * final_gain.astype(jnp.float32)
    saved_states = []
    saved_inputs = []
    saved_acts = []
    outputs = []
    for head_index in range(HEADS):
        embeds = jnp.take(embed_table, next_ids[head_index], axis=0).astype(jnp.float32)
        inputs = (current * rms_scale(current) + embeds).astype(jnp.bfloat16)
        pre_act = jnp.dot(inputs, head_weight[head_index], preferred_element_type=jnp.float32)
        update = jax.nn.silu(pre_act).astype(jnp.bfloat16)
        saved_states.append(current)
        saved_inputs.append(inputs)
        saved_acts.append(pre_act)
        current = current + update.astype(jnp.float32)
        outputs.append(current.astype(jnp.bfloat16))
    gradient = jnp.zeros((TOKENS, D), jnp.float32)
    weight_grads = [None] * HEADS
    for head_index in reversed(range(HEADS)):
        gradient = gradient + state_grad[head_index]
        d_act = (round_trip(gradient) * silu_slope(saved_acts[head_index])).astype(jnp.bfloat16)
        inputs = saved_inputs[head_index]

        def add_group(group_index, running, inputs=inputs, d_act=d_act):
            rows_in = lax.dynamic_slice_in_dim(inputs, group_index * group_rows, group_rows, 0)
            rows_da = lax.dynamic_slice_in_dim(d_act, group_index * group_rows, group_rows, 0)
            return running + round_trip(jnp.dot(rows_in.T, rows_da, preferred_element_type=jnp.float32))
        weight_grads[head_index] = lax.fori_loop(0, N_DP, add_group, jnp.zeros((D, D), jnp.float32))
        if head_index > 0:
            weight = head_weight[head_index]

            def add_columns(block_index, running, weight=weight, d_act=d_act):
                da_part = lax.dynamic_slice_in_dim(d_act, block_index * c_block, c_block, 1)
                w_part = lax.dynamic_slice_in_dim(weight, block_index * c_block, c_block, 1)
                return running + round_trip(jnp.dot(da_part, w_part.T, preferred_element_type=jnp.float32))
            d_input = lax.fori_loop(0, N_TENSOR, add_columns, jnp.zeros((TOKENS, D), jnp.float32))
            previous = saved_states[head_index]
            scale_prev = rms_scale(previous)
            gradient = gradient + scale_prev * d_input - previous * scale_prev ** 3 * lax.optimization_barrier(jnp.mean(d_input * previous, axis=-1, keepdims=True))
    return (jnp.stack(outputs), jnp.stack(weight_grads))
```

```python
import jax
import jax.numpy as jnp
from jax import lax
from jax.sharding import PartitionSpec as P

norm_eps = 1e-06
bf16 = jnp.bfloat16
f32 = jnp.float32


def rms_scale(values):
    return lax.rsqrt(jnp.mean(values * values, axis=-1, keepdims=True) + norm_eps)


def silu_slope(pre_act):
    sigmoid = jax.nn.sigmoid(pre_act)
    return sigmoid * (1.0 + pre_act * (1.0 - sigmoid))


def matmul(left, right, left_dim=1, right_dim=0):
    return lax.dot_general(
        left, right, (((left_dim,), (right_dim,)), ((), ())), preferred_element_type=f32
    )


core_swap = [(index, index ^ 1) for index in range(16)]
same_core = [[2 * chip + core for chip in range(8)] for core in range(2)]
x_lo_swap = [(index, index ^ 1) for index in range(8)]


def to_sibling(values):
    return lax.ppermute(values, "tensor", core_swap)


def exchange(values, split_axis=0, concat_axis=0):
    return lax.all_to_all(
        values,
        "tensor",
        split_axis=split_axis,
        concat_axis=concat_axis,
        tiled=True,
        axis_index_groups=same_core,
    )


def y_send(values, step):
    moves = [(index, (index + 2 * step) % 8) for index in range(8)]
    return lax.ppermute(values, "dp", moves)


def gather_rows(block):
    rows, width = block.shape
    copies = jnp.broadcast_to(block[None], (8, rows, width))
    return exchange(copies).reshape(8 * rows, width)


def scatter_sum(products):
    rows, width = products.shape
    return jnp.sum(exchange(products.reshape(8, rows // 8, width)).astype(f32), axis=0)


def after(values, *earlier):
    return lax.optimization_barrier((values,) + earlier)[0]


def on_device(
    context, residual, out_proj, final_gain, next_ids, embed_table, head_weight, state_grad
):
    tensor_count = lax.axis_size("tensor")
    dp_count = lax.axis_size("dp")
    my_core = lax.axis_index("tensor") % 2
    my_dp = lax.axis_index("dp")
    my_y, my_x = my_dp // 2, my_dp % 2
    first_core = my_core == 0
    tok_rows = residual.shape[0]
    model_width = residual.shape[1]
    head_count, _, head_cols = head_weight.shape
    vocab_rows = embed_table.shape[0]
    table_cols = embed_table.shape[1]
    chip_count = tensor_count // 2

    ids_here = next_ids.reshape(1, -1)
    id_count = ids_here.shape[1]
    group_ids = dp_count * id_count
    capacity = 2 * group_ids // tensor_count
    places_all = tensor_count * capacity
    group = lax.all_to_all(
        jnp.broadcast_to(ids_here, (dp_count, id_count)), "dp", split_axis=0, concat_axis=0, tiled=True
    ).reshape(group_ids)
    owners = group // vocab_rows
    rows_in = group - owners * vocab_rows
    before = jnp.triu(jnp.ones((group_ids, group_ids), bf16), 1)
    is_owner = owners[None, :] == jnp.arange(tensor_count, dtype=jnp.int32)[:, None]
    earlier = matmul(is_owner.astype(bf16), before)
    slots = jnp.sum(jnp.where(is_owner, earlier, 0.0), axis=0).astype(jnp.int32)
    places = owners * capacity + slots
    pick = (places[:, None] == jnp.arange(places_all, dtype=jnp.int32)[None, :]).astype(bf16)
    digits = jnp.stack([rows_in // 64, rows_in % 64]).astype(bf16)
    asked = matmul(digits, pick)
    requests = (asked[0] * 64.0 + asked[1]).astype(jnp.int32).reshape(tensor_count, capacity)
    wanted = lax.all_to_all(requests, "tensor", split_axis=0, concat_axis=0, tiled=True)
    found_rows = jnp.take(embed_table, wanted, axis=0, mode="clip")
    answers = lax.all_to_all(found_rows, "tensor", split_axis=0, concat_axis=0, tiled=True)
    my_rows = matmul(pick, answers.reshape(places_all, table_cols)).astype(bf16)
    my_rows = my_rows.reshape(dp_count, head_count, tok_rows, table_cols)
    spread = lax.all_to_all(my_rows, "dp", split_axis=0, concat_axis=3, tiled=True)
    embeds = spread.reshape(head_count, tok_rows, dp_count * table_cols)

    sibling_weight = to_sibling(head_weight)
    chip_weight = jnp.where(
        first_core,
        jnp.concatenate([head_weight, sibling_weight], axis=2),
        jnp.concatenate([sibling_weight, head_weight], axis=2),
    )

    by_core = context.reshape(chip_count, 2, tok_rows, context.shape[1])
    near_rows = jnp.where(first_core, by_core[:, 0], by_core[:, 1]).reshape(chip_count * tok_rows, -1)
    far_rows = jnp.where(first_core, by_core[:, 1], by_core[:, 0]).reshape(chip_count * tok_rows, -1)
    far = to_sibling(matmul(far_rows, out_proj).astype(bf16))
    near = matmul(near_rows, out_proj).astype(bf16)
    projected = scatter_sum((near.astype(f32) + far.astype(f32)).astype(bf16))
    hidden = residual.astype(f32) + projected
    current = hidden * rms_scale(hidden) * final_gain.astype(f32)
    saved_states = []
    saved_gathered = []
    saved_acts = []
    outputs = []
    for head_index in range(head_count):
        inputs = (current * rms_scale(current) + embeds[head_index].astype(f32)).astype(bf16)
        gathered = gather_rows(inputs)
        pre_act = matmul(gathered, chip_weight[head_index])
        update = jax.nn.silu(pre_act).astype(bf16)
        returned = exchange(update, 0, 1)
        saved_states.append(current)
        saved_gathered.append(gathered)
        saved_acts.append(pre_act)
        current = current + returned.astype(f32)
        outputs.append(current.astype(bf16))

    def chip_rows(head_index, d_act):
        mine = jnp.where(first_core, d_act[:, :head_cols], d_act[:, head_cols:])
        theirs = jnp.where(first_core, d_act[:, head_cols:], d_act[:, :head_cols])
        all_d_act = jnp.concatenate([mine, to_sibling(theirs)], axis=0)
        gathered = saved_gathered[head_index]
        all_inputs = jnp.concatenate([gathered, to_sibling(gathered)], axis=0)
        return all_inputs, all_d_act

    cols = model_width // dp_count
    gradient = jnp.zeros((tok_rows, model_width), f32)
    head_grads = [None] * head_count
    for head_index in reversed(range(head_count)):
        gradient = gradient + state_grad[head_index]
        down_cols = exchange(gradient.astype(bf16), 1, 0)
        d_act = (down_cols.astype(f32) * silu_slope(saved_acts[head_index])).astype(bf16)
        all_inputs, all_d_act = chip_rows(head_index, d_act)
        if head_index > 0:
            d_input = scatter_sum(matmul(d_act, chip_weight[head_index], 1, 1).astype(bf16))
            arrived = []
            for step in range(4):
                target = (my_y + step) % 4
                piece = lax.dynamic_slice_in_dim(all_inputs, target * 2 * cols, 2 * cols, 1)
                product = matmul(piece, all_d_act, 0, 0).astype(bf16)
                arrived.append(y_send(product, step) if step else product)
            total = sum(part.astype(f32) for part in arrived)
            keep = jnp.where(my_x == 0, total[:cols], total[cols:])
            give = jnp.where(my_x == 0, total[cols:], total[:cols]).astype(bf16)
            head_grads[head_index] = keep + lax.ppermute(give, "dp", x_lo_swap).astype(f32)
            previous = saved_states[head_index]
            scale_prev = rms_scale(previous)
            gradient = (
                gradient
                + scale_prev * d_input
                - previous * scale_prev**3 * jnp.mean(d_input * previous, axis=-1, keepdims=True)
            )
        else:
            product = matmul(all_inputs, all_d_act, 0, 0).astype(bf16)
            parts = lax.all_to_all(
                product.reshape(dp_count, cols, head_cols), "dp", split_axis=0, concat_axis=0, tiled=True
            )
            head_grads[head_index] = jnp.sum(parts.astype(f32), axis=0)
    weight_out = jnp.stack(head_grads)
    return (jnp.stack(outputs), weight_out)


def solution(mesh):
    in_specs = (
        P("dp", "tensor"),
        P(("dp", "tensor"), None),
        P("tensor", None),
        P(),
        P(None, ("dp", "tensor")),
        P("tensor", "dp"),
        P(None, None, "tensor"),
        P(None, ("dp", "tensor"), None),
    )
    out_specs = (P(None, ("dp", "tensor"), None), P(None, "dp", "tensor"))
    return jax.shard_map(
        on_device, mesh=mesh, in_specs=in_specs, out_specs=out_specs, check_vma=False
    )
```

```python
import jax
import jax.numpy as jnp
from jax import lax
from jax.experimental import pallas as pl
from jax.experimental.pallas import tpu as pltpu
from jax.sharding import PartitionSpec as P

norm_eps = 1e-06
bf16 = jnp.bfloat16
f32 = jnp.float32
chips = 8
vmem_limit = 16 * 1024 * 1024

steps = [(dz, dx) for dz in range(4) for dx in range(2)]
core_swap = [(index, index ^ 1) for index in range(16)]
same_core = [[2 * chip + core for chip in range(chips)] for core in range(2)]


def chip_moves(axis, dz, dx):
    moves = []
    cores = 2 if axis == "tensor" else 1
    for chip in range(chips):
        target = ((chip // 2 + dz) % 4) * 2 + ((chip % 2) ^ dx)
        for core in range(cores):
            moves.append((chip * cores + core, target * cores + core))
    return moves


def send(values, axis, dz, dx):
    return lax.ppermute(values, axis, chip_moves(axis, dz, dx))


def to_sibling(values):
    return lax.ppermute(values, "tensor", core_swap)


def exchange(values):
    return lax.all_to_all(
        values, "tensor", split_axis=0, concat_axis=0, tiled=True, axis_index_groups=same_core
    )


def gather_chips(block):
    parts = {(0, 0): block}
    parts[(0, 1)] = send(block, "tensor", 0, 1)
    parts[(2, 0)] = send(block, "tensor", 2, 0)
    parts[(1, 0)] = send(block, "tensor", 3, 0)
    parts[(3, 0)] = send(block, "tensor", 1, 0)
    parts[(1, 1)] = send(parts[(0, 1)], "tensor", 3, 0)
    parts[(3, 1)] = send(parts[(0, 1)], "tensor", 1, 0)
    parts[(2, 1)] = send(parts[(2, 0)], "tensor", 0, 1)
    return [parts[step] for step in steps]


def add(*parts):
    total = parts[0].astype(f32)
    for part in parts[1:]:
        total = total + part.astype(f32)
    return total


def scatter_chips(blocks, axis):
    parts = dict(zip(steps, blocks))
    across = send(parts[(2, 1)], axis, 0, 1)
    up = send(parts[(1, 1)], axis, 1, 0)
    down = send(parts[(3, 1)], axis, 3, 0)
    near_up = send(parts[(1, 0)], axis, 1, 0)
    near_down = send(parts[(3, 0)], axis, 3, 0)
    far = send(add(parts[(2, 0)], across).astype(bf16), axis, 2, 0)
    side = send(add(parts[(0, 1)], up, down).astype(bf16), axis, 0, 1)
    return [parts[(0, 0)], near_up, near_down, far, side]


def matmul(left, right, left_dim=1, right_dim=0):
    return lax.dot_general(
        left, right, (((left_dim,), (right_dim,)), ((), ())), preferred_element_type=f32
    )


def call(body, grid, in_specs, out_specs, out_shape, scratch=(), flops=0, moved=0):
    return pl.pallas_call(
        body,
        grid_spec=pltpu.PrefetchScalarGridSpec(
            num_scalar_prefetch=1,
            grid=grid,
            in_specs=in_specs,
            out_specs=out_specs,
            scratch_shapes=list(scratch),
        ),
        out_shape=out_shape,
        compiler_params=pltpu.CompilerParams(vmem_limit_bytes=vmem_limit),
        cost_estimate=pl.CostEstimate(flops=flops, bytes_accessed=moved, transcendentals=0),
    )


def whole():
    return pl.BlockSpec(memory_space=pltpu.VMEM)


def struct(shape, dtype):
    return jax.ShapeDtypeStruct(shape, dtype)


def block_rows(index, rows):
    return pl.ds(pl.multiple_of(index * rows, rows), rows)


def project(place, context, out_proj, rows, far_side, arrived=None):
    depth, width = out_proj.shape
    tile = 1024
    half = chips * rows

    def left(place_ref, context_ref):
        core = place_ref[chips]
        core = 1 - core if far_side else core
        return jnp.concatenate(
            [context_ref[block_rows(place_ref[i] * 2 + core, rows), :] for i in range(chips)], axis=0
        )

    def far_body(place_ref, context_ref, weight_ref, out_ref):
        part = block_rows(pl.program_id(0), tile)
        out_ref[:, part] = matmul(left(place_ref, context_ref), weight_ref[...]).astype(bf16)

    def near_body(place_ref, context_ref, weight_ref, arrived_ref, *out_refs):
        part = block_rows(pl.program_id(0), tile)
        total = matmul(left(place_ref, context_ref), weight_ref[...])
        total = (total + arrived_ref[:, part].astype(f32)).astype(bf16)
        for i in range(chips):
            out_refs[i][:, part] = total[i * rows : (i + 1) * rows]

    in_specs = [whole(), pl.BlockSpec((depth, tile), lambda i, place: (0, i))]
    costs = dict(flops=2 * half * depth * width, moved=2 * depth * width + 4 * half * width)
    if far_side:
        return call(
            far_body, (width // tile,), in_specs, whole(), struct((half, width), bf16), **costs
        )(place, context, out_proj)
    return call(
        near_body,
        (width // tile,),
        in_specs + [whole()],
        [whole()] * chips,
        [struct((rows, width), bf16)] * chips,
        **costs,
    )(place, context, out_proj, arrived)


def forward(place, pieces, weight, sibling, head):
    rows, width = pieces[0].shape
    cols = weight.shape[1]
    tile = 1024
    half = chips * rows
    count = width // tile

    def body(place_ref, *refs):
        piece_refs, (mine_ref, sibling_ref), (update_ref, slope_ref, gathered_ref) = (
            refs[:chips],
            refs[chips : chips + 2],
            refs[chips + 2 : chips + 5],
        )
        mine_acc, sibling_acc = refs[chips + 5 :]
        step = pl.program_id(0)
        part = block_rows(step, tile)
        for i in range(chips):
            gathered_ref[block_rows(place_ref[i], rows), part] = piece_refs[i][:, part]
        left = gathered_ref[:, part]
        mine = matmul(left, mine_ref[0], 1, 1)
        theirs = matmul(left, sibling_ref[0], 1, 1)

        @pl.when(step == 0)
        def _():
            mine_acc[...] = mine
            sibling_acc[...] = theirs

        @pl.when(step > 0)
        def _():
            mine_acc[...] += mine
            sibling_acc[...] += theirs

        @pl.when(step == count - 1)
        def _():
            def results(pre_act):
                sigmoid = 1.0 / (1.0 + jnp.exp(-pre_act))
                return pre_act * sigmoid, sigmoid * (1.0 + pre_act * (1.0 - sigmoid))

            first = place_ref[chips] == 0
            update_a, slope_a = results(mine_acc[...])
            update_b, slope_b = results(sibling_acc[...])
            update_ref[...] = jnp.concatenate(
                [jnp.where(first, update_a, update_b), jnp.where(first, update_b, update_a)], axis=1
            ).astype(bf16)
            slope_ref[...] = jnp.concatenate(
                [jnp.where(first, slope_a, slope_b), jnp.where(first, slope_b, slope_a)], axis=1
            )

    weight_spec = pl.BlockSpec((1, cols, tile), lambda i, place: (head, 0, i))
    return call(
        body,
        (count,),
        [whole()] * chips + [weight_spec] * 2,
        [whole()] * 3,
        [
            struct((half, 2 * cols), bf16),
            struct((half, 2 * cols), f32),
            struct((half, width), bf16),
        ],
        [pltpu.VMEM((half, cols), f32)] * 2,
        flops=4 * half * width * cols,
        moved=4 * width * cols + 4 * half * width,
    )(place, *pieces, weight, sibling)


def slope_product(place, down, slope):
    half, both = slope.shape
    cols = both // 2

    def body(place_ref, down_ref, slope_ref, mine_ref, theirs_ref):
        d_act = down_ref[...].astype(f32) * slope_ref[...]
        first = place_ref[chips] == 0
        low, high = d_act[:, :cols], d_act[:, cols:]
        mine_ref[...] = jnp.where(first, low, high).astype(bf16)
        theirs_ref[...] = jnp.where(first, high, low).astype(bf16)

    return call(
        body,
        (1,),
        [whole()] * 2,
        [whole()] * 2,
        [struct((half, cols), bf16)] * 2,
        moved=half * both * 8,
    )(place, down.reshape(half, both), slope)


def backward(place, mine, theirs, weight, sibling, head):
    half, cols = mine.shape
    width = weight.shape[2]
    rows = half // chips
    tile = 1024

    def body(place_ref, mine_ref, theirs_ref, weight_ref, sibling_ref, *out_refs):
        def ordered(ref):
            return jnp.concatenate([ref[block_rows(place_ref[i], rows), :] for i in range(chips)], axis=0)

        part = block_rows(pl.program_id(0), tile)
        total = matmul(ordered(mine_ref), weight_ref[0])
        total = total + matmul(ordered(theirs_ref), sibling_ref[0])
        total = total.astype(bf16)
        for i in range(chips):
            out_refs[i][:, part] = total[i * rows : (i + 1) * rows]

    weight_spec = pl.BlockSpec((1, cols, tile), lambda i, place: (head, 0, i))
    return call(
        body,
        (width // tile,),
        [whole()] * 2 + [weight_spec] * 2,
        [whole()] * chips,
        [struct((rows, width), bf16)] * chips,
        flops=4 * half * width * cols,
        moved=4 * width * cols + 2 * half * width,
    )(place, mine, theirs, weight, sibling)


def grad_block(target, inputs, sibling_inputs, mine, sibling_mine, cols, dtype):
    half = inputs.shape[0]
    out_rows = mine.shape[1]

    def body(place_ref, inputs_ref, sibling_ref, mine_ref, sibling_mine_ref, out_ref):
        part = block_rows(place_ref[0], cols)
        total = matmul(mine_ref[...], inputs_ref[:, part], 0, 0)
        total = total + matmul(sibling_mine_ref[...], sibling_ref[:, part], 0, 0)
        out_ref[...] = total.astype(dtype)

    return call(
        body,
        (1,),
        [whole()] * 4,
        whole(),
        struct((out_rows, cols), dtype),
        flops=4 * half * cols * out_rows,
        moved=4 * half * (cols + out_rows) + 4 * cols * out_rows,
    )(target.reshape(1), inputs, sibling_inputs, mine, sibling_mine)


def mean_last(values):
    return jnp.mean(values, axis=-1, keepdims=True)


def first_state(place, residual, terms, gain, embeds):
    rows, width = residual.shape
    cols = width // chips

    def body(place_ref, residual_ref, *refs):
        term_refs, gain_ref, embeds_ref, state_ref, inputs_ref = refs[:-4], *refs[-4:]
        hidden = residual_ref[...].astype(f32) + add(*[ref[...] for ref in term_refs])
        state = hidden * lax.rsqrt(mean_last(hidden * hidden) + norm_eps) * gain_ref[...].astype(f32)
        state_ref[...] = state
        scale = lax.rsqrt(mean_last(state * state) + norm_eps)
        for i in range(chips):
            part = slice(i * cols, (i + 1) * cols)
            inputs_ref[:, part] = (state[:, part] * scale + embeds_ref[i].astype(f32)).astype(bf16)

    return call(
        body,
        (1,),
        [whole()] * (3 + len(terms)),
        [whole()] * 2,
        [struct((rows, width), f32), struct((rows, width), bf16)],
        moved=rows * width * 20,
    )(place, residual, *terms, gain.reshape(1, width), embeds)


def next_state(place, state, returned, embeds):
    rows, width = state.shape
    cols = width // chips

    def body(place_ref, state_ref, returned_ref, embeds_ref, state_out, inputs_ref, rounded_ref):
        returned_all = jnp.concatenate([returned_ref[i] for i in range(chips)], axis=1)
        new_state = state_ref[...] + returned_all.astype(f32)
        state_out[...] = new_state
        rounded_ref[...] = new_state.astype(bf16)
        scale = lax.rsqrt(mean_last(new_state * new_state) + norm_eps)
        for i in range(chips):
            part = slice(i * cols, (i + 1) * cols)
            inputs_ref[:, part] = (new_state[:, part] * scale + embeds_ref[i].astype(f32)).astype(bf16)

    return call(
        body,
        (1,),
        [whole()] * 3,
        [whole()] * 3,
        [struct((rows, width), f32), struct((rows, width), bf16), struct((rows, width), bf16)],
        moved=rows * width * 16,
    )(place, state, returned, embeds)


def carry_gradient(place, state_grad, state, terms):
    rows, width = state.shape
    cols = width // chips

    def body(place_ref, upper_ref, lower_ref, state_ref, *refs):
        term_refs, out_ref = refs[:-1], refs[-1]
        previous = state_ref[...]
        d_input = add(*[ref[...] for ref in term_refs])
        scale = lax.rsqrt(mean_last(previous * previous) + norm_eps)
        shared = mean_last(d_input * previous)
        total = upper_ref[0] + scale * d_input - previous * (scale * scale * scale * shared) + lower_ref[0]
        total = total.astype(bf16)
        for i in range(chips):
            out_ref[i] = total[:, i * cols : (i + 1) * cols]

    return call(
        body,
        (1,),
        [
            pl.BlockSpec((1, rows, width), lambda i, place: (1, 0, 0)),
            pl.BlockSpec((1, rows, width), lambda i, place: (0, 0, 0)),
        ]
        + [whole()] * (1 + len(terms)),
        whole(),
        struct((chips, rows, cols), bf16),
        moved=rows * width * 24,
    )(place, state_grad, state_grad, state, *terms)


def after(values, *earlier):
    return lax.optimization_barrier((values,) + earlier)[0]


def on_device(
    context, residual, out_proj, final_gain, next_ids, embed_table, head_weight, state_grad
):
    tensor_count = lax.axis_size("tensor")
    dp_count = lax.axis_size("dp")
    my_tensor = lax.axis_index("tensor")
    my_core = my_tensor % 2
    my_z, my_x_hi = my_tensor // 4, (my_tensor // 2) % 2
    my_dp = lax.axis_index("dp")
    my_y, my_x_lo = my_dp // 2, my_dp % 2
    tok_rows, model_width = residual.shape
    head_count, _, head_cols = head_weight.shape
    weight = jnp.swapaxes(head_weight, 1, 2)
    vocab_rows, table_cols = embed_table.shape
    place = jnp.stack([((my_z + dz) % 4) * 2 + (my_x_hi ^ dx) for dz, dx in steps] + [my_core])
    place = place.astype(jnp.int32)

    ids_here = next_ids.reshape(1, -1)
    id_count = ids_here.shape[1]
    group_ids = dp_count * id_count
    capacity = 2 * group_ids // tensor_count
    places_all = tensor_count * capacity
    group = lax.all_to_all(
        jnp.broadcast_to(ids_here, (dp_count, id_count)), "dp", split_axis=0, concat_axis=0, tiled=True
    )
    group = group.reshape(dp_count, head_count, tok_rows).transpose(1, 0, 2).reshape(group_ids)
    owners = group // vocab_rows
    rows_in = group - owners * vocab_rows
    before = jnp.triu(jnp.ones((group_ids, group_ids), bf16), 1)
    is_owner = owners[None, :] == jnp.arange(tensor_count, dtype=jnp.int32)[:, None]
    earlier = matmul(is_owner.astype(bf16), before)
    slots = jnp.sum(jnp.where(is_owner, earlier, 0.0), axis=0).astype(jnp.int32)
    places = owners * capacity + slots
    pick = (places[:, None] == jnp.arange(places_all, dtype=jnp.int32)[None, :]).astype(bf16)
    digits = jnp.stack([rows_in // 64, rows_in % 64]).astype(bf16)
    asked = matmul(digits, pick)
    requests = (asked[0] * 64.0 + asked[1]).astype(jnp.int32).reshape(tensor_count, capacity)

    arrived = to_sibling(project(place, context, out_proj, tok_rows, True))
    blocks = project(place, context, out_proj, tok_rows, False, arrived)
    requests, blocks = lax.optimization_barrier((requests, blocks))
    terms = scatter_chips(blocks, "tensor")

    wanted = lax.all_to_all(requests, "tensor", split_axis=0, concat_axis=0, tiled=True)
    found_rows = jnp.take(embed_table, wanted, axis=0, mode="clip")
    answers = lax.all_to_all(found_rows, "tensor", split_axis=0, concat_axis=0, tiled=True)
    answers = answers.reshape(places_all, table_cols)
    head_ids = dp_count * tok_rows

    def my_embeds(head):
        rows = matmul(pick[head * head_ids : (head + 1) * head_ids], answers).astype(bf16)
        rows = rows.reshape(dp_count, tok_rows, table_cols)
        return lax.all_to_all(rows, "dp", split_axis=0, concat_axis=0, tiled=True)

    embeds_0 = my_embeds(0)
    sibling_weight = to_sibling(weight)

    state_0, inputs_0 = first_state(place, residual, terms, final_gain, embeds_0)
    pieces_0 = gather_chips(inputs_0)
    answers = after(answers, inputs_0)
    embeds_1 = my_embeds(1)
    update_0, slope_0, gathered_0 = forward(place, pieces_0, weight, sibling_weight, 0)
    returned_0 = exchange(update_0.reshape(chips, tok_rows, 2 * head_cols))
    state_1, inputs_1, rounded_0 = next_state(place, state_0, returned_0, embeds_1)

    pieces_1 = gather_chips(inputs_1)
    upper = state_grad[1].astype(bf16).reshape(tok_rows, chips, 2 * head_cols).transpose(1, 0, 2)
    down_1 = exchange(after(upper, inputs_0))
    update_1, slope_1, gathered_1 = forward(place, pieces_1, weight, sibling_weight, 1)
    mine_1, theirs_1 = slope_product(place, down_1, slope_1)
    d_blocks = backward(place, mine_1, theirs_1, weight, sibling_weight, 1)
    d_terms = scatter_chips(d_blocks, "tensor")

    cols = model_width // dp_count
    sibling_gathered_1 = to_sibling(gathered_1)
    sibling_theirs_1 = to_sibling(theirs_1)
    products = []
    for dy in (2, 1, 3, 0):
        target = ((my_y + dy) % 4).astype(jnp.int32)
        products.append(
            grad_block(target, gathered_1, sibling_gathered_1, mine_1, sibling_theirs_1, 2 * cols, bf16)
        )
    tied = lax.optimization_barrier((d_terms[3], *products))
    d_terms[3], products = tied[0], tied[1:]
    y_terms = [send(part, "dp", dy, 0) for dy, part in zip((2, 1, 3), products)] + [products[3]]
    y_total = add(*y_terms)
    keep = jnp.where(my_x_lo == 0, y_total[:, :cols], y_total[:, cols:])
    give = jnp.where(my_x_lo == 0, y_total[:, cols:], y_total[:, :cols]).astype(bf16)
    grad_1 = keep + send(give, "dp", 0, 1).astype(f32)

    lower = carry_gradient(place, state_grad, state_1, d_terms)
    down_0 = exchange(lower)
    mine_0, theirs_0 = slope_product(place, down_0, slope_0)
    sibling_gathered_0 = to_sibling(gathered_0)
    sibling_theirs_0 = to_sibling(theirs_0)
    grad_blocks = {}
    for step in [(2, 1), (1, 1), (3, 1), (1, 0), (3, 0), (2, 0), (0, 1), (0, 0)]:
        target = (((my_y + step[0]) % 4) * 2 + (my_x_lo ^ step[1])).astype(jnp.int32)
        grad_blocks[step] = grad_block(
            target, gathered_0, sibling_gathered_0, mine_0, sibling_theirs_0, cols, bf16
        )
    grad_0 = add(*scatter_chips([grad_blocks[step] for step in steps], "dp"))

    update_1 = after(update_1, grad_blocks[(0, 0)])
    returned_1 = exchange(update_1.reshape(chips, tok_rows, 2 * head_cols))
    returned_1 = returned_1.transpose(1, 0, 2).reshape(tok_rows, model_width)
    rounded_1 = (state_1 + returned_1.astype(f32)).astype(bf16)
    head_grad = jnp.swapaxes(jnp.stack([grad_0, grad_1]), 1, 2)
    return (jnp.stack([rounded_0, rounded_1]), head_grad)


def solution(mesh):
    in_specs = (
        P("dp", "tensor"),
        P(("dp", "tensor"), None),
        P("tensor", None),
        P(),
        P(None, ("dp", "tensor")),
        P("tensor", "dp"),
        P(None, None, "tensor"),
        P(None, ("dp", "tensor"), None),
    )
    out_specs = (P(None, ("dp", "tensor"), None), P(None, "dp", "tensor"))
    return jax.shard_map(
        on_device, mesh=mesh, in_specs=in_specs, out_specs=out_specs, check_vma=False
    )
```

```python
import jax
import jax.numpy as jnp
from jax import lax
from jax.experimental import pallas as pl
from jax.experimental.pallas import tpu as pltpu
from jax.sharding import PartitionSpec as P

norm_eps = 1e-06
bf16 = jnp.bfloat16
f32 = jnp.float32
chips = 8
mib = 1024 * 1024

steps = [(dz, dx) for dz in range(4) for dx in range(2)]
core_swap = [(index, index ^ 1) for index in range(16)]
same_core = [[2 * chip + core for chip in range(chips)] for core in range(2)]


def chip_moves(axis, dz, dx):
    moves = []
    cores = 2 if axis == "tensor" else 1
    for chip in range(chips):
        target = ((chip // 2 + dz) % 4) * 2 + ((chip % 2) ^ dx)
        for core in range(cores):
            moves.append((chip * cores + core, target * cores + core))
    return moves


def after(values, *earlier):
    return lax.optimization_barrier((values,) + earlier)[0]


def send(values, axis, dz, dx):
    return lax.ppermute(values, axis, chip_moves(axis, dz, dx))


def to_sibling(values):
    return lax.ppermute(values, "tensor", core_swap)


def exchange(values):
    return lax.all_to_all(
        values, "tensor", split_axis=0, concat_axis=0, tiled=True, axis_index_groups=same_core
    )


def gather_chips(block):
    parts = {(0, 0): block}
    parts[(0, 1)] = send(block, "tensor", 0, 1)
    parts[(2, 0)] = send(block, "tensor", 2, 0)
    parts[(1, 0)] = send(block, "tensor", 3, 0)
    parts[(3, 0)] = send(block, "tensor", 1, 0)
    across = after(parts[(0, 1)], parts[(1, 0)], parts[(3, 0)])
    parts[(1, 1)] = send(across, "tensor", 3, 0)
    parts[(3, 1)] = send(across, "tensor", 1, 0)
    parts[(2, 1)] = send(parts[(2, 0)], "tensor", 0, 1)
    return [parts[step] for step in steps]


def add(*parts):
    total = parts[0].astype(f32)
    for part in parts[1:]:
        total = total + part.astype(f32)
    return total


groups = [(0,), (1,), (2, 3), (4,), (5,), (6, 7)]


def scatter_chips(blocks, axis, during=()):
    own, side, up, far, across, down = blocks
    across = send(across, axis, 0, 1)
    up = send(up, axis, 1, 0)
    down = send(down, axis, 3, 0)
    across, up, down, *during = lax.optimization_barrier((across, up, down, *during))
    far = send(add(far, across).astype(bf16), axis, 2, 0)
    side = send(add(side, up[1], down[1]).astype(bf16), axis, 0, 1)
    return [own, up, down, far, side], (across, up, down), during


def matmul(left, right, left_dim=1, right_dim=0):
    return lax.dot_general(
        left, right, (((left_dim,), (right_dim,)), ((), ())), preferred_element_type=f32
    )


def call(body, grid, in_specs, out_specs, out_shape, scratch=(), flops=0, moved=0, limit=16):
    return pl.pallas_call(
        body,
        grid_spec=pltpu.PrefetchScalarGridSpec(
            num_scalar_prefetch=1,
            grid=grid,
            in_specs=in_specs,
            out_specs=out_specs,
            scratch_shapes=list(scratch),
        ),
        out_shape=out_shape,
        compiler_params=pltpu.CompilerParams(vmem_limit_bytes=limit * mib),
        cost_estimate=pl.CostEstimate(flops=flops, bytes_accessed=moved, transcendentals=0),
    )


def whole():
    return pl.BlockSpec(memory_space=pltpu.VMEM)


def in_hbm():
    return pl.BlockSpec(memory_space=pltpu.HBM)


def columns(rows, tile):
    return pl.BlockSpec((rows, tile), lambda i, place: (0, i))


def group_columns(count, rows, tile):
    return pl.BlockSpec((count, rows, tile), lambda i, place: (0, 0, i))


def store_groups(out_refs, total, rows):
    for out_ref, group in zip(out_refs, groups):
        for position, i in enumerate(group):
            out_ref[position] = total[i * rows : (i + 1) * rows]


def struct(shape, dtype):
    return jax.ShapeDtypeStruct(shape, dtype)


def block_rows(index, rows):
    return pl.ds(pl.multiple_of(index * rows, rows), rows)


def project(place, context, out_proj, rows, far_side, arrived=None):
    depth, width = out_proj.shape
    tile = 2560
    half = chips * rows

    def left(place_ref, context_ref):
        core = place_ref[chips]
        core = 1 - core if far_side else core
        return jnp.concatenate(
            [context_ref[block_rows(place_ref[i] * 2 + core, rows), :] for i in range(chips)], axis=0
        )

    def far_body(place_ref, context_ref, weight_ref, out_ref):
        out_ref[...] = matmul(left(place_ref, context_ref), weight_ref[...]).astype(bf16)

    def near_body(place_ref, context_ref, weight_ref, arrived_ref, *out_refs):
        total = matmul(left(place_ref, context_ref), weight_ref[...]) + arrived_ref[...].astype(f32)
        total = total.astype(bf16)
        store_groups(out_refs, total, rows)

    in_specs = [whole(), columns(depth, tile)]
    costs = dict(flops=2 * half * depth * width, moved=2 * depth * width + 4 * half * width)
    if far_side:
        return call(
            far_body,
            (width // tile,),
            in_specs,
            columns(half, tile),
            struct((half, width), bf16),
            **costs,
        )(place, context, out_proj)
    return call(
        near_body,
        (width // tile,),
        in_specs + [columns(half, tile)],
        [group_columns(len(group), rows, tile) for group in groups],
        [struct((len(group), rows, width), bf16) for group in groups],
        limit=60,
        **costs,
    )(place, context, out_proj, arrived)


def forward(place, pieces, weight, sibling, head, extra=None):
    rows, width = pieces[0].shape
    cols = weight.shape[1]
    tile = 2560
    half = chips * rows
    count = width // tile

    def body(place_ref, *refs):
        piece_refs, (mine_ref, sibling_ref) = refs[:chips], refs[chips : chips + 2]
        update_ref, slope_ref, gathered_ref, mine_acc, sibling_acc = refs[-5:]
        step = pl.program_id(0)
        for i in range(chips):
            gathered_ref[block_rows(place_ref[i], rows), :] = piece_refs[i][...]
        left = gathered_ref[...]
        mine = matmul(left, mine_ref[0], 1, 1)
        theirs = matmul(left, sibling_ref[0], 1, 1)

        @pl.when(step == 0)
        def _():
            mine_acc[...] = mine
            sibling_acc[...] = theirs

        @pl.when(step > 0)
        def _():
            mine_acc[...] += mine
            sibling_acc[...] += theirs

        @pl.when(step == count - 1)
        def _():
            def results(pre_act):
                sigmoid = 1.0 / (1.0 + jnp.exp(-pre_act))
                return pre_act * sigmoid, sigmoid * (1.0 + pre_act * (1.0 - sigmoid))

            first = place_ref[chips] == 0
            update_a, slope_a = results(mine_acc[...])
            update_b, slope_b = results(sibling_acc[...])
            update = jnp.concatenate(
                [jnp.where(first, update_a, update_b), jnp.where(first, update_b, update_a)], axis=1
            ).astype(bf16)
            for i in range(chips):
                update_ref[i, :rows] = update[i * rows : (i + 1) * rows]
            if extra is not None:
                update_ref[:, rows:] = refs[chips + 2][...]
            slope_ref[...] = jnp.concatenate(
                [jnp.where(first, slope_a, slope_b), jnp.where(first, slope_b, slope_a)], axis=1
            )

    weight_spec = pl.BlockSpec((1, cols, tile), lambda i, place: (head, 0, i))
    extras = [] if extra is None else [extra]
    update_shape = struct((chips, rows * (1 + len(extras)), 2 * cols), bf16)
    return call(
        body,
        (count,),
        [columns(rows, tile)] * chips + [weight_spec] * 2 + [whole()] * len(extras),
        [whole()] * 2 + [columns(half, tile)],
        [update_shape, struct((half, 2 * cols), f32), struct((half, width), bf16)],
        [pltpu.VMEM((half, cols), f32)] * 2,
        flops=4 * half * width * cols,
        moved=4 * width * cols + 4 * half * width,
        limit=24,
    )(place, *pieces, weight, sibling, *extras)


def split_columns(place, values):
    _, rows, width = values.shape
    cols = width // chips

    def body(place_ref, values_ref, out_ref):
        for i in range(chips):
            out_ref[i] = values_ref[0, :, i * cols : (i + 1) * cols].astype(bf16)

    return call(
        body,
        (1,),
        [pl.BlockSpec((1, rows, width), lambda i, place: (1, 0, 0))],
        whole(),
        struct((chips, rows, cols), bf16),
        moved=rows * width * 6,
    )(place, values)


def slope_product(place, down, slope, start):
    half, both = slope.shape
    cols = both // 2
    rows = half // chips

    def body(place_ref, down_ref, slope_ref, mine_ref, theirs_ref, mine_t_ref, theirs_t_ref):
        d_act = jnp.concatenate([down_ref[i, start : start + rows] for i in range(chips)], axis=0)
        d_act = d_act.astype(f32) * slope_ref[...]
        first = place_ref[chips] == 0
        low, high = d_act[:, :cols], d_act[:, cols:]
        mine = jnp.where(first, low, high)
        theirs = jnp.where(first, high, low)
        mine_ref[...] = mine.astype(bf16)
        theirs_ref[...] = theirs.astype(bf16)
        mine_t_ref[...] = mine.T.astype(bf16)
        theirs_t_ref[...] = theirs.T.astype(bf16)

    return call(
        body,
        (1,),
        [whole()] * 2,
        [whole()] * 4,
        [struct((half, cols), bf16)] * 2 + [struct((cols, half), bf16)] * 2,
        moved=half * both * 8,
    )(place, down, slope)


def backward(place, mine, theirs, weight, sibling, head):
    half, cols = mine.shape
    width = weight.shape[2]
    rows = half // chips
    tile = 2560

    def body(place_ref, mine_ref, theirs_ref, weight_ref, sibling_ref, *out_refs):
        def ordered(ref):
            return jnp.concatenate([ref[block_rows(place_ref[i], rows), :] for i in range(chips)], axis=0)

        total = matmul(ordered(mine_ref), weight_ref[0])
        total = total + matmul(ordered(theirs_ref), sibling_ref[0])
        total = total.astype(bf16)
        store_groups(out_refs, total, rows)

    weight_spec = pl.BlockSpec((1, cols, tile), lambda i, place: (head, 0, i))
    return call(
        body,
        (width // tile,),
        [whole()] * 2 + [weight_spec] * 2,
        [group_columns(len(group), rows, tile) for group in groups],
        [struct((len(group), rows, width), bf16) for group in groups],
        flops=4 * half * width * cols,
        moved=4 * width * cols + 2 * half * width,
    )(place, mine, theirs, weight, sibling)


def grad_blocks(targets, inputs, sibling_inputs, mine, sibling_mine, cols, groups, limit):
    half = inputs.shape[0]
    out_rows = mine.shape[0]
    count = len(targets)

    def body(place_ref, inputs_ref, sibling_ref, mine_ref, sibling_mine_ref, *refs):
        out_refs = refs[: len(groups)]
        right_ref, out_vmem, in_sems, out_sems = refs[len(groups) :]
        homes = {i: out_ref.at[n] for out_ref, group in zip(out_refs, groups) for n, i in enumerate(group)}

        def load(i):
            part = block_rows(place_ref[i], cols)
            return [
                pltpu.make_async_copy(
                    source.at[:, part], right_ref.at[i, pl.ds(j * half, half), :], in_sems.at[i, j]
                )
                for j, source in enumerate((inputs_ref, sibling_ref))
            ]

        def store(i):
            return pltpu.make_async_copy(out_vmem.at[i], homes[i], out_sems.at[i])

        for i in range(count):
            for copy in load(i):
                copy.start()
        left = jnp.concatenate([mine_ref[...], sibling_mine_ref[...]], axis=1)
        for i in range(count):
            for copy in load(i):
                copy.wait()
            out_vmem[i] = matmul(left, right_ref[i]).astype(bf16)
            store(i).start()
        for i in range(count):
            store(i).wait()

    return call(
        body,
        (1,),
        [in_hbm()] * 2 + [whole()] * 2,
        [in_hbm()] * len(groups),
        [struct((len(group), out_rows, cols), bf16) for group in groups],
        [
            pltpu.VMEM((count, 2 * half, cols), bf16),
            pltpu.VMEM((count, out_rows, cols), bf16),
            pltpu.SemaphoreType.DMA((count, 2)),
            pltpu.SemaphoreType.DMA((count,)),
        ],
        flops=4 * half * cols * out_rows * count,
        moved=4 * half * (cols + out_rows) * count + 4 * cols * out_rows * count,
        limit=limit,
    )(jnp.stack(targets).astype(jnp.int32), inputs, sibling_inputs, mine, sibling_mine)


def mean_last(values):
    return jnp.mean(values, axis=-1, keepdims=True)


def first_state(place, residual, terms, gain, embeds):
    rows, width = residual.shape
    cols = width // chips

    def body(place_ref, residual_ref, *refs):
        term_refs, gain_ref, embeds_ref, state_ref, inputs_ref = refs[:-4], *refs[-4:]
        hidden = residual_ref[...].astype(f32) + add(*[ref[0] for ref in term_refs])
        state = hidden * lax.rsqrt(mean_last(hidden * hidden) + norm_eps) * gain_ref[...].astype(f32)
        state_ref[...] = state
        scale = lax.rsqrt(mean_last(state * state) + norm_eps)
        for i in range(chips):
            part = slice(i * cols, (i + 1) * cols)
            inputs_ref[:, part] = (state[:, part] * scale + embeds_ref[i, 0].astype(f32)).astype(bf16)

    return call(
        body,
        (1,),
        [whole()] * (3 + len(terms)),
        [whole()] * 2,
        [struct((rows, width), f32), struct((rows, width), bf16)],
        moved=rows * width * 20,
        limit=60,
    )(place, residual, *terms, gain.reshape(1, width), embeds)


def next_state(place, state, returned, embeds):
    rows, width = state.shape
    cols = width // chips

    def body(place_ref, state_ref, returned_ref, embeds_ref, state_out, inputs_ref, rounded_ref):
        returned_all = jnp.concatenate([returned_ref[i, :rows] for i in range(chips)], axis=1)
        new_state = state_ref[...] + returned_all.astype(f32)
        state_out[...] = new_state
        rounded_ref[...] = new_state.astype(bf16)
        scale = lax.rsqrt(mean_last(new_state * new_state) + norm_eps)
        for i in range(chips):
            part = slice(i * cols, (i + 1) * cols)
            inputs_ref[:, part] = (new_state[:, part] * scale + embeds_ref[i, 1].astype(f32)).astype(bf16)

    return call(
        body,
        (1,),
        [whole()] * 3,
        [whole()] * 3,
        [struct((rows, width), f32), struct((rows, width), bf16), struct((rows, width), bf16)],
        moved=rows * width * 16,
    )(place, state, returned, embeds)


def last_state(place, state, returned):
    rows, width = state.shape
    cols = width // chips

    def body(place_ref, state_ref, returned_ref, out_ref):
        for i in range(chips):
            part = slice(i * cols, (i + 1) * cols)
            out_ref[:, part] = (state_ref[:, part] + returned_ref[i, rows:].astype(f32)).astype(bf16)

    return call(
        body,
        (1,),
        [whole()] * 2,
        whole(),
        struct((rows, width), bf16),
        moved=rows * width * 8,
    )(place, state, returned)


def carry_gradient(place, state_grad, state, terms, extra):
    rows, width = state.shape
    cols = width // chips

    def body(place_ref, upper_ref, lower_ref, state_ref, *refs):
        term_refs, extra_ref, out_ref = refs[:-2], refs[-2], refs[-1]
        previous = state_ref[...]
        d_input = add(*[ref[0] for ref in term_refs])
        scale = lax.rsqrt(mean_last(previous * previous) + norm_eps)
        shared = mean_last(d_input * previous)
        total = upper_ref[0] + scale * d_input - previous * (scale * scale * scale * shared) + lower_ref[0]
        total = total.astype(bf16)
        for i in range(chips):
            out_ref[i, :rows] = total[:, i * cols : (i + 1) * cols]
        out_ref[:, rows:] = extra_ref[...]

    return call(
        body,
        (1,),
        [
            pl.BlockSpec((1, rows, width), lambda i, place: (1, 0, 0)),
            pl.BlockSpec((1, rows, width), lambda i, place: (0, 0, 0)),
        ]
        + [whole()] * (2 + len(terms)),
        whole(),
        struct((chips, 2 * rows, cols), bf16),
        moved=rows * width * 24,
    )(place, state_grad, state_grad, state, *terms, extra)


def on_device(
    context, residual, out_proj, final_gain, next_ids, embed_table, head_weight, state_grad
):
    tensor_count = lax.axis_size("tensor")
    dp_count = lax.axis_size("dp")
    my_tensor = lax.axis_index("tensor")
    my_core = my_tensor % 2
    my_z, my_x_hi = my_tensor // 4, (my_tensor // 2) % 2
    my_dp = lax.axis_index("dp")
    my_y, my_x_lo = my_dp // 2, my_dp % 2
    tok_rows, model_width = residual.shape
    head_count, _, head_cols = head_weight.shape
    weight = jnp.swapaxes(head_weight, 1, 2)
    vocab_rows, table_cols = embed_table.shape
    place = jnp.stack([((my_z + dz) % 4) * 2 + (my_x_hi ^ dx) for dz, dx in steps] + [my_core])
    place = place.astype(jnp.int32)

    ids_here = next_ids.reshape(1, -1)
    id_count = ids_here.shape[1]
    group_ids = dp_count * id_count
    capacity = 2 * group_ids // tensor_count
    places_all = tensor_count * capacity
    group = lax.all_to_all(
        jnp.broadcast_to(ids_here, (dp_count, id_count)), "dp", split_axis=0, concat_axis=0, tiled=True
    )
    group = group.reshape(group_ids)
    owners = group // vocab_rows
    rows_in = group - owners * vocab_rows
    before = jnp.triu(jnp.ones((group_ids, group_ids), bf16), 1)
    is_owner = owners[None, :] == jnp.arange(tensor_count, dtype=jnp.int32)[:, None]
    earlier = matmul(is_owner.astype(bf16), before)
    slots = jnp.sum(jnp.where(is_owner, earlier, 0.0), axis=0).astype(jnp.int32)
    places = owners * capacity + slots
    pick = (places[:, None] == jnp.arange(places_all, dtype=jnp.int32)[None, :]).astype(bf16)
    digits = jnp.stack([rows_in // 64, rows_in % 64]).astype(bf16)
    asked = matmul(digits, pick)
    requests = (asked[0] * 64.0 + asked[1]).astype(jnp.int32).reshape(tensor_count, capacity)

    context = after(context, group)
    arrived = to_sibling(project(place, context, out_proj, tok_rows, True))

    wanted = lax.all_to_all(requests, "tensor", split_axis=0, concat_axis=0, tiled=True)
    found_rows = jnp.take(embed_table, wanted, axis=0, mode="clip")
    arrived = after(arrived, found_rows)
    blocks = project(place, context, out_proj, tok_rows, False, arrived)
    terms, _, _ = scatter_chips(blocks, "tensor")
    answers = lax.all_to_all(found_rows, "tensor", split_axis=0, concat_axis=0, tiled=True)
    answers = answers.reshape(places_all, table_cols)
    my_rows = matmul(pick, answers).astype(bf16)
    my_rows = my_rows.reshape(dp_count, head_count, tok_rows, table_cols)

    embeds = lax.all_to_all(my_rows, "dp", split_axis=0, concat_axis=0, tiled=True)
    sibling_weight = to_sibling(weight)

    state_0, inputs_0 = first_state(place, residual, terms, final_gain, embeds)
    pieces_0 = gather_chips(inputs_0)
    upper = split_columns(place, after(state_grad, inputs_0))
    update_0, slope_0, gathered_0 = forward(place, pieces_0, weight, sibling_weight, 0, upper)
    returned_0 = exchange(update_0)
    state_1, inputs_1, rounded_0 = next_state(place, state_0, returned_0, embeds)

    pieces_1 = gather_chips(inputs_1)
    update_1, slope_1, gathered_1 = forward(place, pieces_1, weight, sibling_weight, 1)
    mine_1, theirs_1, mine_1_t, theirs_1_t = slope_product(place, returned_0, slope_1, tok_rows)
    d_blocks = backward(place, mine_1, theirs_1, weight, sibling_weight, 1)

    cols = model_width // dp_count
    y_targets = [(my_y + dy) % 4 for dy in (2, 1, 3, 0)]
    products = grad_blocks(
        y_targets,
        gathered_1,
        to_sibling(gathered_1),
        mine_1_t,
        to_sibling(theirs_1_t),
        2 * cols,
        [(0,), (1,), (2,), (3,)],
        16,
    )
    d_terms, _, _ = scatter_chips(d_blocks, "tensor", products)
    y_terms = [send(part, "dp", dy, 0) for dy, part in zip((2, 1, 3), products)] + [products[3]]

    lower = carry_gradient(place, state_grad, state_1, d_terms, update_1)
    returned_1 = exchange(lower)
    _, _, mine_0_t, theirs_0_t = slope_product(place, returned_1, slope_0, 0)
    sibling_gathered_0, sibling_0_t = to_sibling(gathered_0), to_sibling(theirs_0_t)

    def made(chosen, mine_t):
        targets = [
            ((my_y + steps[i][0]) % 4) * 2 + (my_x_lo ^ steps[i][1]) for group in chosen for i in group
        ]
        order = iter(range(len(targets)))
        places_of = [tuple(next(order) for _ in group) for group in chosen]
        return grad_blocks(
            targets, gathered_0, sibling_gathered_0, mine_t, sibling_0_t, cols, places_of, 60
        )

    mine_0_t, *y_terms = lax.optimization_barrier((mine_0_t, *y_terms))
    across, up, down = made([(5,), (2, 3), (6, 7)], mine_0_t)
    own, side, far = made([(0,), (1,), (4,)], after(mine_0_t, across))
    y_terms = lax.optimization_barrier((*y_terms, across))[:4]
    y_total = add(*[term[0] for term in y_terms])
    keep = jnp.where(my_x_lo == 0, y_total[:, :cols], y_total[:, cols:])
    give = jnp.where(my_x_lo == 0, y_total[:, cols:], y_total[:, :cols]).astype(bf16)
    given = send(give, "dp", 0, 1)
    grad_terms, first_arrived, (own, side, far, given) = scatter_chips(
        (own, side, up, far, across, down), "dp", (own, side, far, given)
    )
    grad_0 = add(*[term[0] for term in grad_terms])
    grad_1 = keep + given.astype(f32)

    rounded_1 = last_state(place, state_1, after(returned_1, *first_arrived))
    head_grad = jnp.swapaxes(jnp.stack([grad_0, grad_1]), 1, 2)
    return (jnp.stack([rounded_0, rounded_1]), head_grad)


def solution(mesh):
    in_specs = (
        P("dp", "tensor"),
        P(("dp", "tensor"), None),
        P("tensor", None),
        P(),
        P(None, ("dp", "tensor")),
        P("tensor", "dp"),
        P(None, None, "tensor"),
        P(None, ("dp", "tensor"), None),
    )
    out_specs = (P(None, ("dp", "tensor"), None), P(None, "dp", "tensor"))
    return jax.shard_map(
        on_device, mesh=mesh, in_specs=in_specs, out_specs=out_specs, check_vma=False
    )
```

```python
import jax
import jax.numpy as jnp
from jax import lax
from jax.experimental import pallas as pl
from jax.experimental.pallas import tpu as pltpu
from jax.sharding import PartitionSpec as P

norm_eps = 1e-06
bf16 = jnp.bfloat16
f32 = jnp.float32
chips = 8
mib = 1024 * 1024

steps = [(dz, dx) for dz in range(4) for dx in range(2)]
core_swap = [(index, index ^ 1) for index in range(16)]
same_core = [[2 * chip + core for chip in range(chips)] for core in range(2)]


def chip_moves(axis, dz, dx):
    moves = []
    cores = 2 if axis == "tensor" else 1
    for chip in range(chips):
        target = ((chip // 2 + dz) % 4) * 2 + ((chip % 2) ^ dx)
        for core in range(cores):
            moves.append((chip * cores + core, target * cores + core))
    return moves


def after(values, *earlier):
    return lax.optimization_barrier((values,) + earlier)[0]


def send(values, axis, dz, dx):
    return lax.ppermute(values, axis, chip_moves(axis, dz, dx))


def to_sibling(values):
    return lax.ppermute(values, "tensor", core_swap)


def exchange(values):
    return lax.all_to_all(
        values, "tensor", split_axis=0, concat_axis=0, tiled=True, axis_index_groups=same_core
    )


def gather_chips(block):
    parts = {(0, 0): block}
    parts[(0, 1)] = send(block, "tensor", 0, 1)
    parts[(2, 0)] = send(block, "tensor", 2, 0)
    parts[(1, 0)] = send(block, "tensor", 3, 0)
    parts[(3, 0)] = send(block, "tensor", 1, 0)
    across = after(parts[(0, 1)], parts[(1, 0)], parts[(3, 0)])
    parts[(1, 1)] = send(across, "tensor", 3, 0)
    parts[(3, 1)] = send(across, "tensor", 1, 0)
    parts[(2, 1)] = send(parts[(2, 0)], "tensor", 0, 1)
    return [parts[step] for step in steps]


def add(*parts):
    total = parts[0].astype(f32)
    for part in parts[1:]:
        total = total + part.astype(f32)
    return total


groups = [(0,), (1,), (2, 3), (4,), (5,), (6, 7)]


def scatter_chips(blocks, axis, during=()):
    own, side, up, far, across, down = blocks
    across = send(across, axis, 0, 1)
    up = send(up, axis, 1, 0)
    down = send(down, axis, 3, 0)
    across, up, down, *during = lax.optimization_barrier((across, up, down, *during))
    far = send(add(far, across).astype(bf16), axis, 2, 0)
    side = send(add(side, up[1], down[1]).astype(bf16), axis, 0, 1)
    return [own, up, down, far, side], (across, up, down), during


def matmul(left, right, left_dim=1, right_dim=0):
    return lax.dot_general(
        left, right, (((left_dim,), (right_dim,)), ((), ())), preferred_element_type=f32
    )


def call(body, grid, in_specs, out_specs, out_shape, scratch=(), flops=0, moved=0, limit=16):
    return pl.pallas_call(
        body,
        grid_spec=pltpu.PrefetchScalarGridSpec(
            num_scalar_prefetch=1,
            grid=grid,
            in_specs=in_specs,
            out_specs=out_specs,
            scratch_shapes=list(scratch),
        ),
        out_shape=out_shape,
        compiler_params=pltpu.CompilerParams(vmem_limit_bytes=limit * mib),
        cost_estimate=pl.CostEstimate(flops=flops, bytes_accessed=moved, transcendentals=0),
    )


def whole():
    return pl.BlockSpec(memory_space=pltpu.VMEM)


def in_hbm():
    return pl.BlockSpec(memory_space=pltpu.HBM)


def columns(rows, tile):
    return pl.BlockSpec((rows, tile), lambda i, place: (0, i))


def group_columns(count, rows, tile):
    return pl.BlockSpec((count, rows, tile), lambda i, place: (0, 0, i))


def store_groups(out_refs, total, rows):
    for out_ref, group in zip(out_refs, groups):
        for position, i in enumerate(group):
            out_ref[position] = total[i * rows : (i + 1) * rows]


def struct(shape, dtype):
    return jax.ShapeDtypeStruct(shape, dtype)


def block_rows(index, rows):
    return pl.ds(pl.multiple_of(index * rows, rows), rows)


def project(place, context, out_proj, rows, far_side, arrived=None):
    depth, width = out_proj.shape
    tile = 2560
    half = chips * rows

    def left(place_ref, context_ref):
        core = place_ref[chips]
        core = 1 - core if far_side else core
        return jnp.concatenate(
            [context_ref[block_rows(place_ref[i] * 2 + core, rows), :] for i in range(chips)], axis=0
        )

    def far_body(place_ref, context_ref, weight_ref, out_ref):
        out_ref[...] = matmul(left(place_ref, context_ref), weight_ref[...]).astype(bf16)

    def near_body(place_ref, context_ref, weight_ref, arrived_ref, *out_refs):
        total = matmul(left(place_ref, context_ref), weight_ref[...]) + arrived_ref[...].astype(f32)
        total = total.astype(bf16)
        store_groups(out_refs, total, rows)

    in_specs = [whole(), columns(depth, tile)]
    costs = dict(flops=2 * half * depth * width, moved=2 * depth * width + 4 * half * width)
    if far_side:
        return call(
            far_body,
            (width // tile,),
            in_specs,
            columns(half, tile),
            struct((half, width), bf16),
            **costs,
        )(place, context, out_proj)
    return call(
        near_body,
        (width // tile,),
        in_specs + [columns(half, tile)],
        [group_columns(len(group), rows, tile) for group in groups],
        [struct((len(group), rows, width), bf16) for group in groups],
        limit=60,
        **costs,
    )(place, context, out_proj, arrived)


def forward(place, pieces, weight, sibling, head, extra):
    rows, width = pieces[0].shape
    cols = weight.shape[1]
    tile = 2560
    half = chips * rows
    count = width // tile

    def body(place_ref, *refs):
        piece_refs, (mine_ref, sibling_ref) = refs[:chips], refs[chips : chips + 2]
        update_ref, slope_ref, gathered_ref, mine_acc, sibling_acc = refs[-5:]
        step = pl.program_id(0)
        for i in range(chips):
            gathered_ref[block_rows(place_ref[i], rows), :] = piece_refs[i][...]
        left = gathered_ref[...]
        mine = matmul(left, mine_ref[0], 1, 1)
        theirs = matmul(left, sibling_ref[0], 1, 1)

        @pl.when(step == 0)
        def _():
            mine_acc[...] = mine
            sibling_acc[...] = theirs

        @pl.when(step > 0)
        def _():
            mine_acc[...] += mine
            sibling_acc[...] += theirs

        @pl.when(step == count - 1)
        def _():
            def results(pre_act):
                sigmoid = 1.0 / (1.0 + jnp.exp(-pre_act))
                return pre_act * sigmoid, sigmoid * (1.0 + pre_act * (1.0 - sigmoid))

            first = place_ref[chips] == 0
            update_a, slope_a = results(mine_acc[...])
            update_b, slope_b = results(sibling_acc[...])
            update = jnp.concatenate(
                [jnp.where(first, update_a, update_b), jnp.where(first, update_b, update_a)], axis=1
            ).astype(bf16)
            for i in range(chips):
                update_ref[i, :rows] = update[i * rows : (i + 1) * rows]
            update_ref[:, rows:] = refs[chips + 2][...]
            slope_ref[...] = jnp.concatenate(
                [jnp.where(first, slope_a, slope_b), jnp.where(first, slope_b, slope_a)], axis=1
            )

    weight_spec = pl.BlockSpec((1, cols, tile), lambda i, place: (head, 0, i))
    update_shape = struct((chips, 2 * rows, 2 * cols), bf16)
    return call(
        body,
        (count,),
        [columns(rows, tile)] * chips + [weight_spec] * 2 + [whole()],
        [whole()] * 2 + [columns(half, tile)],
        [update_shape, struct((half, 2 * cols), f32), struct((half, width), bf16)],
        [pltpu.VMEM((half, cols), f32)] * 2,
        flops=4 * half * width * cols,
        moved=4 * width * cols + 4 * half * width,
        limit=24,
    )(place, *pieces, weight, sibling, extra)


def forward_backward(place, pieces, weight, sibling, head, down):
    rows, width = pieces[0].shape
    cols = weight.shape[1]
    tile = 2560
    half = chips * rows
    count = width // tile

    def body(place_ref, *refs):
        piece_refs, (mine_ref, sibling_ref, down_ref) = refs[:chips], refs[chips : chips + 3]
        update_ref, mine_t_ref, theirs_t_ref, gathered_ref = refs[chips + 3 : chips + 7]
        out_refs = refs[chips + 7 : -2]
        mine_acc, sibling_acc = refs[-2:]
        step = pl.program_id(0)

        @pl.when(step < count)
        def _():
            for i in range(chips):
                gathered_ref[block_rows(place_ref[i], rows), :] = piece_refs[i][...]
            left = gathered_ref[...]
            mine = matmul(left, mine_ref[0], 1, 1)
            theirs = matmul(left, sibling_ref[0], 1, 1)

            @pl.when(step == 0)
            def _():
                mine_acc[...] = mine
                sibling_acc[...] = theirs

            @pl.when(step > 0)
            def _():
                mine_acc[...] += mine
                sibling_acc[...] += theirs

        @pl.when(step == count - 1)
        def _():
            first = place_ref[chips] == 0
            down_all = jnp.concatenate([down_ref[i, rows:] for i in range(chips)], axis=0).astype(f32)
            low, high = down_all[:, :cols], down_all[:, cols:]

            def results(acc, down_cols, out_t_ref):
                pre_act = acc[...]
                sigmoid = 1.0 / (1.0 + jnp.exp(-pre_act))
                d_act = down_cols * (sigmoid * (1.0 + pre_act * (1.0 - sigmoid)))
                acc[...] = d_act
                out_t_ref[...] = d_act.T.astype(bf16)
                return pre_act * sigmoid

            update_a = results(mine_acc, jnp.where(first, low, high), mine_t_ref)
            update_b = results(sibling_acc, jnp.where(first, high, low), theirs_t_ref)
            update = jnp.concatenate(
                [jnp.where(first, update_a, update_b), jnp.where(first, update_b, update_a)], axis=1
            ).astype(bf16)
            for i in range(chips):
                update_ref[i] = update[i * rows : (i + 1) * rows]

        @pl.when(step >= count)
        def _():
            def ordered(ref):
                parts = [ref[block_rows(place_ref[i], rows), :] for i in range(chips)]
                return jnp.concatenate(parts, axis=0).astype(bf16)

            total = matmul(ordered(mine_acc), mine_ref[0])
            total = total + matmul(ordered(sibling_acc), sibling_ref[0])
            store_groups(out_refs, total.astype(bf16), rows)

    def there(i):
        return jnp.minimum(i, count - 1)

    def back(i):
        return jnp.where(i < count, count - 1, 2 * count - 1 - i)

    def both_ways(i):
        return jnp.where(i < count, i, 2 * count - 1 - i)

    weight_spec = pl.BlockSpec((1, cols, tile), lambda i, place: (head, 0, both_ways(i)))
    return call(
        body,
        (2 * count,),
        [pl.BlockSpec((rows, tile), lambda i, place: (0, there(i)))] * chips
        + [weight_spec] * 2
        + [whole()],
        [whole()] * 3
        + [pl.BlockSpec((half, tile), lambda i, place: (0, there(i)))]
        + [pl.BlockSpec((len(g), rows, tile), lambda i, place: (0, 0, back(i))) for g in groups],
        [
            struct((chips, rows, 2 * cols), bf16),
            struct((cols, half), bf16),
            struct((cols, half), bf16),
            struct((half, width), bf16),
        ]
        + [struct((len(g), rows, width), bf16) for g in groups],
        [pltpu.VMEM((half, cols), f32)] * 2,
        flops=8 * half * width * cols,
        moved=6 * width * cols + 6 * half * width,
        limit=36,
    )(place, *pieces, weight, sibling, down)


def split_columns(place, values):
    _, rows, width = values.shape
    cols = width // chips

    def body(place_ref, values_ref, out_ref):
        for i in range(chips):
            out_ref[i] = values_ref[0, :, i * cols : (i + 1) * cols].astype(bf16)

    return call(
        body,
        (1,),
        [pl.BlockSpec((1, rows, width), lambda i, place: (1, 0, 0))],
        whole(),
        struct((chips, rows, cols), bf16),
        moved=rows * width * 6,
    )(place, values)


def slope_product(place, down, slope):
    half, both = slope.shape
    cols = both // 2
    rows = half // chips

    def body(place_ref, down_ref, slope_ref, mine_ref, theirs_ref):
        d_act = jnp.concatenate([down_ref[i, :rows] for i in range(chips)], axis=0)
        d_act = d_act.astype(f32) * slope_ref[...]
        first = place_ref[chips] == 0
        low, high = d_act[:, :cols], d_act[:, cols:]
        mine_ref[...] = jnp.where(first, low, high).T.astype(bf16)
        theirs_ref[...] = jnp.where(first, high, low).T.astype(bf16)

    return call(
        body,
        (1,),
        [whole()] * 2,
        [whole()] * 2,
        [struct((cols, half), bf16)] * 2,
        moved=half * both * 8,
    )(place, down, slope)


def grad_blocks(place, targets, inputs, sibling_inputs, mine, sibling_mine, cols, groups, limit):
    half = inputs.shape[0]
    out_rows = mine.shape[0]
    count = len(targets)

    def body(place_ref, inputs_ref, sibling_ref, mine_ref, sibling_mine_ref, *refs):
        out_refs = refs[: len(groups)]
        right_ref, out_vmem, in_sems, out_sems = refs[len(groups) :]
        homes = {i: out_ref.at[n] for out_ref, group in zip(out_refs, groups) for n, i in enumerate(group)}

        def load(i):
            part = block_rows(place_ref[targets[i]], cols)
            return [
                pltpu.make_async_copy(
                    source.at[:, part], right_ref.at[i, pl.ds(j * half, half), :], in_sems.at[i, j]
                )
                for j, source in enumerate((inputs_ref, sibling_ref))
            ]

        def store(i):
            return pltpu.make_async_copy(out_vmem.at[i], homes[i], out_sems.at[i])

        for i in range(count):
            for copy in load(i):
                copy.start()
        left = jnp.concatenate([mine_ref[...], sibling_mine_ref[...]], axis=1)
        for i in range(count):
            for copy in load(i):
                copy.wait()
            out_vmem[i] = matmul(left, right_ref[i]).astype(bf16)
            store(i).start()
        for i in range(count):
            store(i).wait()

    return call(
        body,
        (1,),
        [in_hbm()] * 2 + [whole()] * 2,
        [in_hbm()] * len(groups),
        [struct((len(group), out_rows, cols), bf16) for group in groups],
        [
            pltpu.VMEM((count, 2 * half, cols), bf16),
            pltpu.VMEM((count, out_rows, cols), bf16),
            pltpu.SemaphoreType.DMA((count, 2)),
            pltpu.SemaphoreType.DMA((count,)),
        ],
        flops=4 * half * cols * out_rows * count,
        moved=4 * half * (cols + out_rows) * count + 4 * cols * out_rows * count,
        limit=limit,
    )(place, inputs, sibling_inputs, mine, sibling_mine)


def mean_last(values):
    return jnp.mean(values, axis=-1, keepdims=True)


def first_state(place, residual, terms, gain, embeds):
    rows, width = residual.shape
    cols = width // chips

    def body(place_ref, residual_ref, *refs):
        term_refs, gain_ref, embeds_ref, state_ref, inputs_ref = refs[:-4], *refs[-4:]
        hidden = residual_ref[...].astype(f32) + add(*[ref[0] for ref in term_refs])
        state = hidden * lax.rsqrt(mean_last(hidden * hidden) + norm_eps) * gain_ref[...].astype(f32)
        state_ref[...] = state
        scale = lax.rsqrt(mean_last(state * state) + norm_eps)
        for i in range(chips):
            part = slice(i * cols, (i + 1) * cols)
            inputs_ref[:, part] = (state[:, part] * scale + embeds_ref[i, 0].astype(f32)).astype(bf16)

    return call(
        body,
        (1,),
        [whole()]
        + [pl.BlockSpec((1, rows, width), lambda i, place: (0, 0, 0))] * len(terms)
        + [whole(), pl.BlockSpec((chips, 1, rows, cols), lambda i, place: (0, 0, 0, 0))],
        [whole()] * 2,
        [struct((rows, width), f32), struct((rows, width), bf16)],
        moved=rows * width * 20,
        limit=60,
    )(place, residual, *terms, gain.reshape(1, width), embeds)


def next_state(place, state, returned, embeds):
    rows, width = state.shape
    cols = width // chips

    def body(place_ref, state_ref, returned_ref, embeds_ref, state_out, inputs_ref, rounded_ref):
        returned_all = jnp.concatenate([returned_ref[i, :rows] for i in range(chips)], axis=1)
        new_state = state_ref[...] + returned_all.astype(f32)
        state_out[...] = new_state
        rounded_ref[...] = new_state.astype(bf16)
        scale = lax.rsqrt(mean_last(new_state * new_state) + norm_eps)
        for i in range(chips):
            part = slice(i * cols, (i + 1) * cols)
            inputs_ref[:, part] = (new_state[:, part] * scale + embeds_ref[i, 1].astype(f32)).astype(bf16)

    return call(
        body,
        (1,),
        [whole()] * 3,
        [whole()] * 3,
        [struct((rows, width), f32), struct((rows, width), bf16), struct((rows, width), bf16)],
        moved=rows * width * 16,
    )(place, state, returned, embeds)


def both_states(place, rounded, state, returned):
    rows, width = state.shape
    cols = width // chips

    def body(place_ref, rounded_ref, state_ref, returned_ref, out_ref):
        out_ref[0] = rounded_ref[...]
        for i in range(chips):
            part = slice(i * cols, (i + 1) * cols)
            out_ref[1, :, part] = (state_ref[:, part] + returned_ref[i, rows:].astype(f32)).astype(bf16)

    return call(
        body,
        (1,),
        [whole()] * 3,
        whole(),
        struct((2, rows, width), bf16),
        moved=rows * width * 12,
    )(place, rounded, state, returned)


def carry_gradient(place, state_grad, state, terms, extra):
    rows, width = state.shape
    cols = width // chips

    def body(place_ref, upper_ref, lower_ref, state_ref, *refs):
        term_refs, extra_ref, out_ref = refs[:-2], refs[-2], refs[-1]
        previous = state_ref[...]
        d_input = add(*[ref[0] for ref in term_refs])
        scale = lax.rsqrt(mean_last(previous * previous) + norm_eps)
        shared = mean_last(d_input * previous)
        total = upper_ref[0] + scale * d_input - previous * (scale * scale * scale * shared) + lower_ref[0]
        total = total.astype(bf16)
        for i in range(chips):
            out_ref[i, :rows] = total[:, i * cols : (i + 1) * cols]
        out_ref[:, rows:] = extra_ref[...]

    return call(
        body,
        (1,),
        [
            pl.BlockSpec((1, rows, width), lambda i, place: (1, 0, 0)),
            pl.BlockSpec((1, rows, width), lambda i, place: (0, 0, 0)),
        ]
        + [whole()] * (2 + len(terms)),
        whole(),
        struct((chips, 2 * rows, cols), bf16),
        moved=rows * width * 24,
    )(place, state_grad, state_grad, state, *terms, extra)


def on_device(
    context, residual, out_proj, final_gain, next_ids, embed_table, head_weight, state_grad
):
    tensor_count = lax.axis_size("tensor")
    dp_count = lax.axis_size("dp")
    my_tensor = lax.axis_index("tensor")
    my_core = my_tensor % 2
    my_z, my_x_hi = my_tensor // 4, (my_tensor // 2) % 2
    my_dp = lax.axis_index("dp")
    my_y, my_x_lo = my_dp // 2, my_dp % 2
    tok_rows, model_width = residual.shape
    head_count, _, head_cols = head_weight.shape
    weight = jnp.swapaxes(head_weight, 1, 2)
    vocab_rows, table_cols = embed_table.shape
    place = jnp.stack(
        [((my_z + dz) % 4) * 2 + (my_x_hi ^ dx) for dz, dx in steps]
        + [my_core]
        + [((my_y + dy) % 4) * 2 + (my_x_lo ^ dx) for dy, dx in steps]
        + [(my_y + dy) % 4 for dy in range(4)]
    )
    place = place.astype(jnp.int32)

    ids_here = next_ids.reshape(1, -1)
    id_count = ids_here.shape[1]
    group_ids = dp_count * id_count
    capacity = 2 * group_ids // tensor_count
    places_all = tensor_count * capacity
    group = lax.all_to_all(
        jnp.broadcast_to(ids_here, (dp_count, id_count)), "dp", split_axis=0, concat_axis=0, tiled=True
    )
    group = group.reshape(group_ids)
    owners = group // vocab_rows
    rows_in = group - owners * vocab_rows
    before = jnp.triu(jnp.ones((group_ids, group_ids), bf16), 1)
    is_owner = owners[None, :] == jnp.arange(tensor_count, dtype=jnp.int32)[:, None]
    earlier = matmul(is_owner.astype(bf16), before)
    slots = jnp.sum(jnp.where(is_owner, earlier, 0.0), axis=0).astype(jnp.int32)
    places = owners * capacity + slots
    pick = (places[:, None] == jnp.arange(places_all, dtype=jnp.int32)[None, :]).astype(bf16)
    digits = jnp.stack([rows_in // 64, rows_in % 64]).astype(bf16)
    asked = matmul(digits, pick)
    requests = (asked[0] * 64.0 + asked[1]).astype(jnp.int32).reshape(tensor_count, capacity)

    context = after(context, group)
    arrived = to_sibling(project(place, context, out_proj, tok_rows, True))

    wanted = lax.all_to_all(requests, "tensor", split_axis=0, concat_axis=0, tiled=True)
    found_rows = jnp.take(embed_table, wanted, axis=0, mode="clip")
    arrived = after(arrived, found_rows)
    blocks = project(place, context, out_proj, tok_rows, False, arrived)
    terms, _, _ = scatter_chips(blocks, "tensor")
    answers = lax.all_to_all(found_rows, "tensor", split_axis=0, concat_axis=0, tiled=True)
    answers = answers.reshape(places_all, table_cols)
    my_rows = matmul(pick, answers).astype(bf16)
    my_rows = my_rows.reshape(dp_count, head_count, tok_rows, table_cols)

    embeds = lax.all_to_all(my_rows, "dp", split_axis=0, concat_axis=0, tiled=True)
    sibling_weight = to_sibling(weight)

    state_0, inputs_0 = first_state(place, residual, terms, final_gain, embeds)
    pieces_0 = gather_chips(inputs_0)
    upper = split_columns(place, after(state_grad, inputs_0))
    update_0, slope_0, gathered_0 = forward(place, pieces_0, weight, sibling_weight, 0, upper)
    returned_0 = exchange(update_0)
    state_1, inputs_1, rounded_0 = next_state(place, state_0, returned_0, embeds)

    pieces_1 = gather_chips(inputs_1)
    update_1, mine_1_t, theirs_1_t, gathered_1, *d_blocks = forward_backward(
        place, pieces_1, weight, sibling_weight, 1, returned_0
    )

    cols = model_width // dp_count
    y_targets = [2 * chips + 1 + dy for dy in (2, 1, 3, 0)]
    products = grad_blocks(
        place,
        y_targets,
        gathered_1,
        to_sibling(gathered_1),
        mine_1_t,
        to_sibling(theirs_1_t),
        2 * cols,
        [(0,), (1,), (2,), (3,)],
        16,
    )
    d_terms, _, _ = scatter_chips(d_blocks, "tensor", products)
    y_terms = [send(part, "dp", dy, 0) for dy, part in zip((2, 1, 3), products)] + [products[3]]

    lower = carry_gradient(place, state_grad, state_1, d_terms, update_1)
    returned_1 = exchange(lower)
    mine_0_t, theirs_0_t = slope_product(place, returned_1, slope_0)
    sibling_gathered_0, sibling_0_t = to_sibling(gathered_0), to_sibling(theirs_0_t)

    def made(chosen, mine_t):
        targets = [chips + 1 + i for group in chosen for i in group]
        order = iter(range(len(targets)))
        places_of = [tuple(next(order) for _ in group) for group in chosen]
        return grad_blocks(
            place, targets, gathered_0, sibling_gathered_0, mine_t, sibling_0_t, cols, places_of, 60
        )

    mine_0_t, y_terms[1], y_terms[2] = lax.optimization_barrier((mine_0_t, y_terms[1], y_terms[2]))
    across, up, down = made([(5,), (2, 3), (6, 7)], mine_0_t)
    own, side, far = made([(0,), (1,), (4,)], after(mine_0_t, across))
    y_terms = lax.optimization_barrier((*y_terms, across))[:4]
    y_total = add(*[term[0] for term in y_terms])
    keep = jnp.where(my_x_lo == 0, y_total[:, :cols], y_total[:, cols:])
    give = jnp.where(my_x_lo == 0, y_total[:, cols:], y_total[:, :cols]).astype(bf16)
    given = send(give, "dp", 0, 1)
    states = both_states(place, rounded_0, state_1, returned_1)
    grad_terms, _, (own, side, far, given, states) = scatter_chips(
        (own, side, up, far, across, down), "dp", (own, side, far, given, states)
    )
    grad_0 = add(*[term[0] for term in grad_terms])
    grad_1 = keep + given.astype(f32)

    head_grad = jnp.swapaxes(jnp.stack([grad_0, grad_1]), 1, 2)
    return (states, head_grad)


def solution(mesh):
    in_specs = (
        P("dp", "tensor"),
        P(("dp", "tensor"), None),
        P("tensor", None),
        P(),
        P(None, ("dp", "tensor")),
        P("tensor", "dp"),
        P(None, None, "tensor"),
        P(None, ("dp", "tensor"), None),
    )
    out_specs = (P(None, ("dp", "tensor"), None), P(None, "dp", "tensor"))
    return jax.shard_map(
        on_device, mesh=mesh, in_specs=in_specs, out_specs=out_specs, check_vma=False
    )
```

```python
import jax
import jax.numpy as jnp
from jax import lax
from jax.experimental import pallas as pl
from jax.experimental.pallas import tpu as pltpu
from jax.sharding import PartitionSpec as P

norm_eps = 1e-06
bf16 = jnp.bfloat16
f32 = jnp.float32
chips = 8
mib = 1024 * 1024

steps = [(dz, dx) for dz in range(4) for dx in range(2)]
core_swap = [(index, index ^ 1) for index in range(16)]
same_core = [[2 * chip + core for chip in range(chips)] for core in range(2)]


def chip_moves(axis, dz, dx):
    moves = []
    cores = 2 if axis == "tensor" else 1
    for chip in range(chips):
        target = ((chip // 2 + dz) % 4) * 2 + ((chip % 2) ^ dx)
        for core in range(cores):
            moves.append((chip * cores + core, target * cores + core))
    return moves


def after(values, *earlier):
    return lax.optimization_barrier((values,) + earlier)[0]


def send(values, axis, dz, dx):
    return lax.ppermute(values, axis, chip_moves(axis, dz, dx))


def to_sibling(values):
    return lax.ppermute(values, "tensor", core_swap)


def exchange(values):
    return lax.all_to_all(
        values, "tensor", split_axis=0, concat_axis=0, tiled=True, axis_index_groups=same_core
    )


def gather_chips(block):
    parts = {(0, 0): block}
    parts[(0, 1)] = send(block, "tensor", 0, 1)
    parts[(2, 0)] = send(block, "tensor", 2, 0)
    parts[(1, 0)] = send(block, "tensor", 3, 0)
    parts[(3, 0)] = send(block, "tensor", 1, 0)
    across = after(parts[(0, 1)], parts[(1, 0)], parts[(3, 0)])
    parts[(1, 1)] = send(across, "tensor", 3, 0)
    parts[(3, 1)] = send(across, "tensor", 1, 0)
    parts[(2, 1)] = send(parts[(2, 0)], "tensor", 0, 1)
    return [parts[step] for step in steps]


def add(*parts):
    total = parts[0].astype(f32)
    for part in parts[1:]:
        total = total + part.astype(f32)
    return total


groups = [(0,), (1,), (2, 3), (4,), (5,), (6, 7)]


def scatter_chips(blocks, axis, during=()):
    own, side, up, far, across, down = blocks
    across = send(across, axis, 0, 1)
    up = send(up, axis, 1, 0)
    down = send(down, axis, 3, 0)
    across, up, down, *during = lax.optimization_barrier((across, up, down, *during))
    far = send(add(far, across).astype(bf16), axis, 2, 0)
    side = send(add(side, up[1], down[1]).astype(bf16), axis, 0, 1)
    return [own, up, down, far, side], (across, up, down), during


def matmul(left, right, left_dim=1, right_dim=0):
    return lax.dot_general(
        left, right, (((left_dim,), (right_dim,)), ((), ())), preferred_element_type=f32
    )


def call(body, grid, in_specs, out_specs, out_shape, scratch=(), flops=0, moved=0, limit=16):
    return pl.pallas_call(
        body,
        grid_spec=pltpu.PrefetchScalarGridSpec(
            num_scalar_prefetch=1,
            grid=grid,
            in_specs=in_specs,
            out_specs=out_specs,
            scratch_shapes=list(scratch),
        ),
        out_shape=out_shape,
        compiler_params=pltpu.CompilerParams(vmem_limit_bytes=limit * mib),
        cost_estimate=pl.CostEstimate(flops=flops, bytes_accessed=moved, transcendentals=0),
    )


def whole():
    return pl.BlockSpec(memory_space=pltpu.VMEM)


def in_hbm():
    return pl.BlockSpec(memory_space=pltpu.HBM)


def columns(rows, tile):
    return pl.BlockSpec((rows, tile), lambda i, place: (0, i))


def group_columns(count, rows, tile):
    return pl.BlockSpec((count, rows, tile), lambda i, place: (0, 0, i))


def store_groups(out_refs, total, rows):
    for out_ref, group in zip(out_refs, groups):
        for position, i in enumerate(group):
            out_ref[position] = total[i * rows : (i + 1) * rows]


def struct(shape, dtype):
    return jax.ShapeDtypeStruct(shape, dtype)


def block_rows(index, rows):
    return pl.ds(pl.multiple_of(index * rows, rows), rows)


def project(place, context, out_proj, rows, far_side, arrived=None):
    depth, width = out_proj.shape
    tile = 2560
    half = chips * rows

    def left(place_ref, context_ref):
        core = place_ref[chips]
        core = 1 - core if far_side else core
        return jnp.concatenate(
            [context_ref[block_rows(place_ref[i] * 2 + core, rows), :] for i in range(chips)], axis=0
        )

    def far_body(place_ref, context_ref, weight_ref, out_ref):
        out_ref[...] = matmul(left(place_ref, context_ref), weight_ref[...]).astype(bf16)

    def near_body(place_ref, context_ref, weight_ref, arrived_ref, *out_refs):
        total = matmul(left(place_ref, context_ref), weight_ref[...]) + arrived_ref[...].astype(f32)
        total = total.astype(bf16)
        store_groups(out_refs, total, rows)

    in_specs = [whole(), columns(depth, tile)]
    costs = dict(flops=2 * half * depth * width, moved=2 * depth * width + 4 * half * width)
    if far_side:
        return call(
            far_body,
            (width // tile,),
            in_specs,
            columns(half, tile),
            struct((half, width), bf16),
            **costs,
        )(place, context, out_proj)
    return call(
        near_body,
        (width // tile,),
        in_specs + [columns(half, tile)],
        [group_columns(len(group), rows, tile) for group in groups],
        [struct((len(group), rows, width), bf16) for group in groups],
        limit=60,
        **costs,
    )(place, context, out_proj, arrived)


def forward(place, pieces, weight, sibling, head, extra):
    rows, width = pieces[0].shape
    cols = weight.shape[1]
    tile = 2560
    half = chips * rows
    count = width // tile

    def body(place_ref, *refs):
        piece_refs, (mine_ref, sibling_ref) = refs[:chips], refs[chips : chips + 2]
        update_ref, slope_ref, gathered_ref, mine_acc, sibling_acc = refs[-5:]
        step = pl.program_id(0)
        for i in range(chips):
            gathered_ref[block_rows(place_ref[i], rows), :] = piece_refs[i][...]
        left = gathered_ref[...]
        mine = matmul(left, mine_ref[0], 1, 1)
        theirs = matmul(left, sibling_ref[0], 1, 1)

        @pl.when(step == 0)
        def _():
            mine_acc[...] = mine
            sibling_acc[...] = theirs

        @pl.when(step > 0)
        def _():
            mine_acc[...] += mine
            sibling_acc[...] += theirs

        @pl.when(step == count - 1)
        def _():
            def results(pre_act):
                sigmoid = 1.0 / (1.0 + jnp.exp(-pre_act))
                return pre_act * sigmoid, sigmoid * (1.0 + pre_act * (1.0 - sigmoid))

            first = place_ref[chips] == 0
            update_a, slope_a = results(mine_acc[...])
            update_b, slope_b = results(sibling_acc[...])
            update = jnp.concatenate(
                [jnp.where(first, update_a, update_b), jnp.where(first, update_b, update_a)], axis=1
            ).astype(bf16)
            for i in range(chips):
                update_ref[i, :rows] = update[i * rows : (i + 1) * rows]
            update_ref[:, rows:] = refs[chips + 2][...]
            slope_ref[...] = jnp.concatenate(
                [jnp.where(first, slope_a, slope_b), jnp.where(first, slope_b, slope_a)], axis=1
            )

    weight_spec = pl.BlockSpec((1, cols, tile), lambda i, place: (head, 0, i))
    update_shape = struct((chips, 2 * rows, 2 * cols), bf16)
    return call(
        body,
        (count,),
        [columns(rows, tile)] * chips + [weight_spec] * 2 + [whole()],
        [whole()] * 2 + [columns(half, tile)],
        [update_shape, struct((half, 2 * cols), f32), struct((half, width), bf16)],
        [pltpu.VMEM((half, cols), f32)] * 2,
        flops=4 * half * width * cols,
        moved=4 * width * cols + 4 * half * width,
        limit=24,
    )(place, *pieces, weight, sibling, extra)


def forward_backward(place, pieces, weight, sibling, head, down):
    rows, width = pieces[0].shape
    cols = weight.shape[1]
    tile = 2560
    half = chips * rows
    count = width // tile

    def body(place_ref, *refs):
        piece_refs, (mine_ref, sibling_ref, down_ref) = refs[:chips], refs[chips : chips + 3]
        update_ref, mine_t_ref, theirs_t_ref, gathered_ref = refs[chips + 3 : chips + 7]
        out_refs = refs[chips + 7 : -2]
        mine_acc, sibling_acc = refs[-2:]
        step = pl.program_id(0)

        @pl.when(step < count)
        def _():
            for i in range(chips):
                gathered_ref[block_rows(place_ref[i], rows), :] = piece_refs[i][...]
            left = gathered_ref[...]
            mine = matmul(left, mine_ref[0], 1, 1)
            theirs = matmul(left, sibling_ref[0], 1, 1)

            @pl.when(step == 0)
            def _():
                mine_acc[...] = mine
                sibling_acc[...] = theirs

            @pl.when(step > 0)
            def _():
                mine_acc[...] += mine
                sibling_acc[...] += theirs

        @pl.when(step == count - 1)
        def _():
            first = place_ref[chips] == 0
            down_all = jnp.concatenate([down_ref[i, rows:] for i in range(chips)], axis=0).astype(f32)
            low, high = down_all[:, :cols], down_all[:, cols:]

            def results(acc, down_cols, out_t_ref):
                pre_act = acc[...]
                sigmoid = 1.0 / (1.0 + jnp.exp(-pre_act))
                d_act = down_cols * (sigmoid * (1.0 + pre_act * (1.0 - sigmoid)))
                acc[...] = d_act
                out_t_ref[...] = d_act.T.astype(bf16)
                return pre_act * sigmoid

            update_a = results(mine_acc, jnp.where(first, low, high), mine_t_ref)
            update_b = results(sibling_acc, jnp.where(first, high, low), theirs_t_ref)
            update = jnp.concatenate(
                [jnp.where(first, update_a, update_b), jnp.where(first, update_b, update_a)], axis=1
            ).astype(bf16)
            for i in range(chips):
                update_ref[i] = update[i * rows : (i + 1) * rows]

        @pl.when(step >= count)
        def _():
            def ordered(ref):
                parts = [ref[block_rows(place_ref[i], rows), :] for i in range(chips)]
                return jnp.concatenate(parts, axis=0).astype(bf16)

            total = matmul(ordered(mine_acc), mine_ref[0])
            total = total + matmul(ordered(sibling_acc), sibling_ref[0])
            store_groups(out_refs, total.astype(bf16), rows)

    def there(i):
        return jnp.minimum(i, count - 1)

    def back(i):
        return jnp.where(i < count, count - 1, 2 * count - 1 - i)

    def both_ways(i):
        return jnp.where(i < count, i, 2 * count - 1 - i)

    weight_spec = pl.BlockSpec((1, cols, tile), lambda i, place: (head, 0, both_ways(i)))
    return call(
        body,
        (2 * count,),
        [pl.BlockSpec((rows, tile), lambda i, place: (0, there(i)))] * chips
        + [weight_spec] * 2
        + [whole()],
        [whole()] * 3
        + [pl.BlockSpec((half, tile), lambda i, place: (0, there(i)))]
        + [pl.BlockSpec((len(g), rows, tile), lambda i, place: (0, 0, back(i))) for g in groups],
        [
            struct((chips, rows, 2 * cols), bf16),
            struct((cols, half), bf16),
            struct((cols, half), bf16),
            struct((half, width), bf16),
        ]
        + [struct((len(g), rows, width), bf16) for g in groups],
        [pltpu.VMEM((half, cols), f32)] * 2,
        flops=8 * half * width * cols,
        moved=6 * width * cols + 6 * half * width,
        limit=36,
    )(place, *pieces, weight, sibling, down)


def split_columns(place, values):
    _, rows, width = values.shape
    cols = width // chips

    def body(place_ref, values_ref, out_ref):
        for i in range(chips):
            out_ref[i] = values_ref[0, :, i * cols : (i + 1) * cols].astype(bf16)

    return call(
        body,
        (1,),
        [pl.BlockSpec((1, rows, width), lambda i, place: (1, 0, 0))],
        whole(),
        struct((chips, rows, cols), bf16),
        moved=rows * width * 6,
    )(place, values)


def slope_product(place, down, slope):
    half, both = slope.shape
    cols = both // 2
    rows = half // chips

    def body(place_ref, down_ref, slope_ref, mine_ref, theirs_ref):
        d_act = jnp.concatenate([down_ref[i, :rows] for i in range(chips)], axis=0)
        d_act = d_act.astype(f32) * slope_ref[...]
        first = place_ref[chips] == 0
        low, high = d_act[:, :cols], d_act[:, cols:]
        mine_ref[...] = jnp.where(first, low, high).T.astype(bf16)
        theirs_ref[...] = jnp.where(first, high, low).T.astype(bf16)

    return call(
        body,
        (1,),
        [whole()] * 2,
        [whole()] * 2,
        [struct((cols, half), bf16)] * 2,
        moved=half * both * 8,
    )(place, down, slope)


def grad_blocks(place, targets, inputs, sibling_inputs, mine, sibling_mine, cols, groups, limit):
    half = inputs.shape[0]
    out_rows = mine.shape[0]
    count = len(targets)

    def body(place_ref, inputs_ref, sibling_ref, mine_ref, sibling_mine_ref, *refs):
        out_refs = refs[: len(groups)]
        right_ref, out_vmem, in_sems, out_sems = refs[len(groups) :]
        homes = {i: out_ref.at[n] for out_ref, group in zip(out_refs, groups) for n, i in enumerate(group)}

        def load(i):
            part = block_rows(place_ref[targets[i]], cols)
            return [
                pltpu.make_async_copy(
                    source.at[:, part], right_ref.at[i, pl.ds(j * half, half), :], in_sems.at[i, j]
                )
                for j, source in enumerate((inputs_ref, sibling_ref))
            ]

        def store(i):
            return pltpu.make_async_copy(out_vmem.at[i], homes[i], out_sems.at[i])

        for i in range(count):
            for copy in load(i):
                copy.start()
        left = jnp.concatenate([mine_ref[...], sibling_mine_ref[...]], axis=1)
        for i in range(count):
            for copy in load(i):
                copy.wait()
            out_vmem[i] = matmul(left, right_ref[i]).astype(bf16)
            store(i).start()
        for i in range(count):
            store(i).wait()

    return call(
        body,
        (1,),
        [in_hbm()] * 2 + [whole()] * 2,
        [in_hbm()] * len(groups),
        [struct((len(group), out_rows, cols), bf16) for group in groups],
        [
            pltpu.VMEM((count, 2 * half, cols), bf16),
            pltpu.VMEM((count, out_rows, cols), bf16),
            pltpu.SemaphoreType.DMA((count, 2)),
            pltpu.SemaphoreType.DMA((count,)),
        ],
        flops=4 * half * cols * out_rows * count,
        moved=4 * half * (cols + out_rows) * count + 4 * cols * out_rows * count,
        limit=limit,
    )(place, inputs, sibling_inputs, mine, sibling_mine)


def mean_last(values):
    return jnp.mean(values, axis=-1, keepdims=True)


def first_state(place, residual, terms, gain, embeds):
    rows, width = residual.shape
    cols = width // chips

    def body(place_ref, residual_ref, *refs):
        term_refs, gain_ref, embeds_ref, state_ref, inputs_ref = refs[:-4], *refs[-4:]
        hidden = residual_ref[...].astype(f32) + add(*[ref[0] for ref in term_refs])
        state = hidden * lax.rsqrt(mean_last(hidden * hidden) + norm_eps) * gain_ref[...].astype(f32)
        state_ref[...] = state
        scale = lax.rsqrt(mean_last(state * state) + norm_eps)
        for i in range(chips):
            part = slice(i * cols, (i + 1) * cols)
            inputs_ref[:, part] = (state[:, part] * scale + embeds_ref[i, 0].astype(f32)).astype(bf16)

    return call(
        body,
        (1,),
        [whole()]
        + [pl.BlockSpec((1, rows, width), lambda i, place: (0, 0, 0))] * len(terms)
        + [whole(), pl.BlockSpec((chips, 1, rows, cols), lambda i, place: (0, 0, 0, 0))],
        [whole()] * 2,
        [struct((rows, width), f32), struct((rows, width), bf16)],
        moved=rows * width * 20,
        limit=60,
    )(place, residual, *terms, gain.reshape(1, width), embeds)


def next_state(place, state, returned, embeds):
    rows, width = state.shape
    cols = width // chips

    def body(place_ref, state_ref, returned_ref, embeds_ref, state_out, inputs_ref, rounded_ref):
        returned_all = jnp.concatenate([returned_ref[i, :rows] for i in range(chips)], axis=1)
        new_state = state_ref[...] + returned_all.astype(f32)
        state_out[...] = new_state
        rounded_ref[...] = new_state.astype(bf16)
        scale = lax.rsqrt(mean_last(new_state * new_state) + norm_eps)
        for i in range(chips):
            part = slice(i * cols, (i + 1) * cols)
            inputs_ref[:, part] = (new_state[:, part] * scale + embeds_ref[i, 1].astype(f32)).astype(bf16)

    return call(
        body,
        (1,),
        [whole()] * 3,
        [whole()] * 3,
        [struct((rows, width), f32), struct((rows, width), bf16), struct((rows, width), bf16)],
        moved=rows * width * 16,
    )(place, state, returned, embeds)


def both_states(place, rounded, state, returned):
    rows, width = state.shape
    cols = width // chips

    def body(place_ref, rounded_ref, state_ref, returned_ref, out_ref):
        out_ref[0] = rounded_ref[...]
        for i in range(chips):
            part = slice(i * cols, (i + 1) * cols)
            out_ref[1, :, part] = (state_ref[:, part] + returned_ref[i, rows:].astype(f32)).astype(bf16)

    return call(
        body,
        (1,),
        [whole()] * 3,
        whole(),
        struct((2, rows, width), bf16),
        moved=rows * width * 12,
    )(place, rounded, state, returned)


def carry_gradient(place, state_grad, state, terms, extra):
    rows, width = state.shape
    cols = width // chips

    def body(place_ref, upper_ref, lower_ref, state_ref, *refs):
        term_refs, extra_ref, out_ref = refs[:-2], refs[-2], refs[-1]
        previous = state_ref[...]
        d_input = add(*[ref[0] for ref in term_refs])
        scale = lax.rsqrt(mean_last(previous * previous) + norm_eps)
        shared = mean_last(d_input * previous)
        total = upper_ref[0] + scale * d_input - previous * (scale * scale * scale * shared) + lower_ref[0]
        total = total.astype(bf16)
        for i in range(chips):
            out_ref[i, :rows] = total[:, i * cols : (i + 1) * cols]
        out_ref[:, rows:] = extra_ref[...]

    return call(
        body,
        (1,),
        [
            pl.BlockSpec((1, rows, width), lambda i, place: (1, 0, 0)),
            pl.BlockSpec((1, rows, width), lambda i, place: (0, 0, 0)),
        ]
        + [whole()] * (2 + len(terms)),
        whole(),
        struct((chips, 2 * rows, cols), bf16),
        moved=rows * width * 24,
    )(place, state_grad, state_grad, state, *terms, extra)


def swap_ids(ids, axis):
    count, width = ids.shape
    tiles = jnp.pad(ids, ((0, 0), (0, 128 - width)))
    tiles = jnp.broadcast_to(tiles[:, None, :], (count, 8, 128))
    tiles = lax.all_to_all(tiles, axis, split_axis=0, concat_axis=0, tiled=True)
    return tiles[:, 0, :width]


def on_device(
    context, residual, out_proj, final_gain, next_ids, embed_table, head_weight, state_grad
):
    tensor_count = lax.axis_size("tensor")
    dp_count = lax.axis_size("dp")
    my_tensor = lax.axis_index("tensor")
    my_core = my_tensor % 2
    my_z, my_x_hi = my_tensor // 4, (my_tensor // 2) % 2
    my_dp = lax.axis_index("dp")
    my_y, my_x_lo = my_dp // 2, my_dp % 2
    tok_rows, model_width = residual.shape
    head_count, _, head_cols = head_weight.shape
    weight = jnp.swapaxes(head_weight, 1, 2)
    vocab_rows, table_cols = embed_table.shape
    place = jnp.stack(
        [((my_z + dz) % 4) * 2 + (my_x_hi ^ dx) for dz, dx in steps]
        + [my_core]
        + [((my_y + dy) % 4) * 2 + (my_x_lo ^ dx) for dy, dx in steps]
        + [(my_y + dy) % 4 for dy in range(4)]
    )
    place = place.astype(jnp.int32)

    ids_here = next_ids.reshape(1, -1)
    id_count = ids_here.shape[1]
    group_ids = dp_count * id_count
    capacity = 2 * group_ids // tensor_count
    places_all = tensor_count * capacity
    group = swap_ids(jnp.broadcast_to(ids_here, (dp_count, id_count)), "dp")
    group = group.reshape(group_ids)
    owners = group // vocab_rows
    rows_in = group - owners * vocab_rows
    before = jnp.triu(jnp.ones((group_ids, group_ids), bf16), 1)
    is_owner = owners[None, :] == jnp.arange(tensor_count, dtype=jnp.int32)[:, None]
    earlier = matmul(is_owner.astype(bf16), before)
    slots = jnp.sum(jnp.where(is_owner, earlier, 0.0), axis=0).astype(jnp.int32)
    places = owners * capacity + slots
    pick = (places[:, None] == jnp.arange(places_all, dtype=jnp.int32)[None, :]).astype(bf16)
    digits = jnp.stack([rows_in // 64, rows_in % 64]).astype(bf16)
    asked = matmul(digits, pick)
    requests = (asked[0] * 64.0 + asked[1]).astype(jnp.int32).reshape(tensor_count, capacity)

    context = after(context, group)
    arrived = to_sibling(project(place, context, out_proj, tok_rows, True))

    wanted = swap_ids(requests, "tensor")
    found_rows = jnp.take(embed_table, wanted, axis=0, mode="clip")
    arrived = after(arrived, found_rows)
    blocks = project(place, context, out_proj, tok_rows, False, arrived)
    terms, _, _ = scatter_chips(blocks, "tensor")
    answers = lax.all_to_all(found_rows, "tensor", split_axis=0, concat_axis=0, tiled=True)
    answers = answers.reshape(places_all, table_cols)
    my_rows = matmul(pick, answers).astype(bf16)
    my_rows = my_rows.reshape(dp_count, head_count, tok_rows, table_cols)

    embeds = lax.all_to_all(my_rows, "dp", split_axis=0, concat_axis=0, tiled=True)
    sibling_weight = to_sibling(weight)

    state_0, inputs_0 = first_state(place, residual, terms, final_gain, embeds)
    pieces_0 = gather_chips(inputs_0)
    upper = split_columns(place, after(state_grad, inputs_0))
    update_0, slope_0, gathered_0 = forward(place, pieces_0, weight, sibling_weight, 0, upper)
    returned_0 = exchange(update_0)
    state_1, inputs_1, rounded_0 = next_state(place, state_0, returned_0, embeds)

    pieces_1 = gather_chips(inputs_1)
    update_1, mine_1_t, theirs_1_t, gathered_1, *d_blocks = forward_backward(
        place, pieces_1, weight, sibling_weight, 1, returned_0
    )

    cols = model_width // dp_count
    y_targets = [2 * chips + 1 + dy for dy in (2, 1, 3, 0)]
    products = grad_blocks(
        place,
        y_targets,
        gathered_1,
        to_sibling(gathered_1),
        mine_1_t,
        to_sibling(theirs_1_t),
        2 * cols,
        [(0,), (1,), (2,), (3,)],
        16,
    )
    d_terms, _, _ = scatter_chips(d_blocks, "tensor", products)
    y_terms = [send(part, "dp", dy, 0) for dy, part in zip((2, 1, 3), products)] + [products[3]]

    lower = carry_gradient(place, state_grad, state_1, d_terms, update_1)
    returned_1 = exchange(lower)
    mine_0_t, theirs_0_t = slope_product(place, returned_1, slope_0)
    sibling_gathered_0, sibling_0_t = to_sibling(gathered_0), to_sibling(theirs_0_t)

    def made(chosen, mine_t):
        targets = [chips + 1 + i for group in chosen for i in group]
        order = iter(range(len(targets)))
        places_of = [tuple(next(order) for _ in group) for group in chosen]
        return grad_blocks(
            place, targets, gathered_0, sibling_gathered_0, mine_t, sibling_0_t, cols, places_of, 60
        )

    mine_0_t, y_terms[1], y_terms[2] = lax.optimization_barrier((mine_0_t, y_terms[1], y_terms[2]))
    across, up, down = made([(5,), (2, 3), (6, 7)], mine_0_t)
    own, side, far = made([(0,), (1,), (4,)], after(mine_0_t, across))
    y_terms = lax.optimization_barrier((*y_terms, across))[:4]
    y_total = add(*[term[0] for term in y_terms])
    keep = jnp.where(my_x_lo == 0, y_total[:, :cols], y_total[:, cols:])
    give = jnp.where(my_x_lo == 0, y_total[:, cols:], y_total[:, :cols]).astype(bf16)
    given = send(give, "dp", 0, 1)
    states = both_states(place, rounded_0, state_1, returned_1)
    grad_terms, _, (own, side, far, given, states) = scatter_chips(
        (own, side, up, far, across, down), "dp", (own, side, far, given, states)
    )
    grad_0 = add(*[term[0] for term in grad_terms])
    grad_1 = keep + given.astype(f32)

    head_grad = jnp.swapaxes(jnp.stack([grad_0, grad_1]), 1, 2)
    return (states, head_grad)


def solution(mesh):
    in_specs = (
        P("dp", "tensor"),
        P(("dp", "tensor"), None),
        P("tensor", None),
        P(),
        P(None, ("dp", "tensor")),
        P("tensor", "dp"),
        P(None, None, "tensor"),
        P(None, ("dp", "tensor"), None),
    )
    out_specs = (P(None, ("dp", "tensor"), None), P(None, "dp", "tensor"))
    return jax.shard_map(
        on_device, mesh=mesh, in_specs=in_specs, out_specs=out_specs, check_vma=False
    )
```
